128 devices in a mesh: row: 8 (over y_hi, z), col: 16 (over x, y_lo, core).
Axes of the slice: x: 4, y: 4 (y_hi: 2, y_lo: 2; y = y_hi * 2 + y_lo), z: 4, core: 2. Of those that a mesh axis runs over, the one named last changes fastest.
Arguments:
- tiles: bfloat16 [8, 16, 512, 128, 128], P('row', 'col'), may hold values from -0.125 to 0.125
- tile_coords: int32 [8, 16, 512, 2], P('row', 'col'), may hold values from 0 to 255, as said below
- tile_counts: int32 [8, 16], P('row', 'col'), may hold values from 128 to 512, as said below
- omega: bfloat16 [64, 262144], P(None, 'col'), may hold values from -6 to 6
Outputs:
- sketch: float32 [64, 262144], P(None, 'col')
The draws below stay inside these ranges and needn't reach their ends.
Inputs may be any that keep to these rules, and one draw needn't show every extreme that they name: `tile_coords`: within one device the 512 slots name distinct blocks; block rows lie in 0 to 255 and block columns in 0 to 127. `tile_counts`: each count is 512, 256 or 128.
All inputs are finite; a program needn't handle non-finite values.
Results may differ from the reference program's by a relative error of at most 0.0021.
Values may be sent and summed in bfloat16 or wider, within the bound.
No kernel may reach another device: no remote copies, remote signals or barrier semaphores. Data moves between devices by JAX's collectives and lax.ppermute only.
A program may use at most 128 MiB of HBM per device.

```python
import jax
import jax.numpy as jnp
from jax import lax

TILE = 128
COLS = 64
BLK_COL = 128
CAP = 512
BLK_ROW = 256
NODES = 262144
N_ROW = 8
N_COL = 16


def draw_tile_coords(key, part):
    key = jax.random.fold_in(key, 11)
    slots_all = BLK_ROW * BLK_COL
    keys = jax.random.split(key, N_ROW * N_COL)

    def one_device(sub):
        first, second = jax.random.split(sub)
        inner_slots = jax.random.permutation(first, slots_all - 2)[:CAP - 2] + 1
        chosen = jnp.concatenate([jnp.array([0, slots_all - 1], jnp.int32), inner_slots.astype(jnp.int32)])
        return jax.random.permutation(second, chosen)
    slots = jax.vmap(one_device)(keys)
    coords = jnp.stack([slots // BLK_COL, slots % BLK_COL], axis=-1)
    return coords.reshape(N_ROW, N_COL, CAP, 2).astype(jnp.int32)


def draw_tile_counts(key, part):
    key = jax.random.fold_in(key, 12)
    first, second, third = jax.random.split(key, 3)
    number = N_ROW * N_COL
    levels = jax.random.randint(first, (number,), 0, 3)
    counts = jnp.full((number,), CAP, jnp.int32) // jnp.left_shift(jnp.ones((number,), jnp.int32), levels)
    top_place = jax.random.randint(second, (), 0, number)
    low_place = (top_place + 1 + jax.random.randint(third, (), 0, number - 1)) % number
    counts = counts.at[top_place].set(CAP)
    counts = counts.at[low_place].set(CAP // 4)
    return counts.reshape(N_ROW, N_COL).astype(jnp.int32)


def block_levels(rng, extent, pieces, smallest, high):
    gain = 1.0
    for position, parts in pieces:
        draws = jax.random.uniform(jax.random.fold_in(jax.random.fold_in(rng, 6), position), (parts,), jnp.float32, smallest / len(pieces), high / len(pieces))
        gain = gain * jnp.repeat(jnp.exp(draws), extent[position] // parts).reshape((-1,) + (1,) * (len(extent) - 1 - position))
    return gain


def bell_draw(key, extent, scale, bound, pieces=(), kind=jnp.bfloat16):
    gain = block_levels(key, extent, pieces, -0.22, 0.18) if pieces else 1.0
    values = jax.random.normal(key, extent, jnp.float32) * scale * gain
    return jnp.minimum(jnp.maximum(values, -bound), bound).astype(kind)


def setup_inputs(seed: int = 0) -> dict:
    key_list = jax.random.split(jax.random.key(seed), 5)
    return {
        "tiles": bell_draw(key_list[0], (N_ROW, N_COL, CAP, TILE, TILE), (CAP * N_COL * 64 // BLK_ROW) ** -0.5, 0.125, ((0, 8), (1, 16))),
        "tile_coords": draw_tile_coords(jax.random.fold_in(key_list[4], 71), 0),
        "tile_counts": draw_tile_counts(jax.random.fold_in(key_list[4], 71), 0),
        "omega": bell_draw(key_list[3], (COLS, NODES), 1.0, 6.0, ((1, 16),)),
    }


def reference(tiles, tile_coords, tile_counts, omega):
    devices_all = N_ROW * N_COL
    row_blocks = BLK_ROW * N_ROW
    col_blocks = BLK_COL * N_COL
    flat_tiles = tiles.reshape(devices_all, CAP, TILE, TILE)
    flat_coords = tile_coords.reshape(devices_all, CAP, 2)
    flat_counts = tile_counts.reshape(devices_all)
    index_all = jnp.arange(devices_all, dtype=jnp.int32)
    slot_index = jnp.arange(CAP, dtype=jnp.int32)
    omega_blocks = omega.reshape(COLS, col_blocks, TILE).transpose(1, 0, 2).astype(jnp.float32)

    def forward(carry, item):
        blocks, coords, count, device = item
        grid_row = device // N_COL
        grid_col = device % N_COL
        live = (slot_index < count).astype(jnp.float32)
        rows_global = grid_row * BLK_ROW + coords[:, 0]
        cols_global = grid_col * BLK_COL + coords[:, 1]
        picked = omega_blocks[cols_global]
        prod = jnp.einsum("kcb,krb->kcr", picked, blocks.astype(jnp.float32)) * live[:, None, None]
        return carry + jax.ops.segment_sum(prod, rows_global, num_segments=row_blocks), None

    inner, _ = lax.scan(forward, jnp.zeros((row_blocks, COLS, TILE), jnp.float32),
                        (flat_tiles, flat_coords, flat_counts, index_all))
    inner = inner.astype(jnp.bfloat16).astype(jnp.float32)

    def backward(carry, item):
        blocks, coords, count, device = item
        grid_row = device // N_COL
        grid_col = device % N_COL
        live = (slot_index < count).astype(jnp.float32)
        rows_global = grid_row * BLK_ROW + coords[:, 0]
        cols_global = grid_col * BLK_COL + coords[:, 1]
        picked = inner[rows_global]
        prod = jnp.einsum("kcr,krb->kcb", picked, blocks.astype(jnp.float32)) * live[:, None, None]
        return carry + jax.ops.segment_sum(prod, cols_global, num_segments=col_blocks), None

    outer, _ = lax.scan(backward, jnp.zeros((col_blocks, COLS, TILE), jnp.float32),
                        (flat_tiles, flat_coords, flat_counts, index_all))
    return outer.transpose(1, 0, 2).reshape(COLS, NODES)
```

```python
import functools

import jax
import jax.numpy as jnp
from jax import lax
from jax.experimental import pallas as pl
from jax.experimental.pallas import tpu as pltpu
from jax.sharding import Mesh
from jax.sharding import PartitionSpec as P

TILE = 128
CHUNK = 32
UNROLL = 4
LEVEL = 32700.0
STEPS = 8.0
VMEM = 56 * 1024 * 1024
ROW = ("yh", "z")
CHIPS = ("x", "yl")
F32 = jnp.float32
I16 = jnp.int16


def params():
    return pltpu.CompilerParams(vmem_limit_bytes=VMEM)


def code(block):
    top = jnp.maximum(jnp.max(jnp.abs(block), axis=0, keepdims=True), 1e-30)
    step = jnp.ceil(jnp.log2(top) * STEPS)
    return step, jnp.exp2(step * (-1.0 / STEPS)) * LEVEL


def factor(step):
    return jnp.exp2(step * (1.0 / STEPS)) * (1.0 / LEVEL)


def put_block(block, piece, j, out_ref, steps):
    width = block.shape[0]
    step, gain = code(block)
    whole = jnp.round(block * gain).astype(jnp.int32)
    out_ref[piece, pl.ds(pl.multiple_of(j * width, width), width), :] = whole.astype(I16)
    steps[piece, pl.ds(j, 1), :] = step


def live_chunks(count):
    return lax.div(count + (CHUNK - 1), CHUNK)


def sparse_step(transposed, coords, base, source, tiles_ref, acc):
    def body(i, _):
        products = []
        for u in range(UNROLL):
            k = i * UNROLL + u
            slot = base + k
            r, c = coords[2 * slot], coords[2 * slot + 1]
            if transposed:
                left = source[:, pl.ds(pl.multiple_of(c * TILE, TILE), TILE)]
                value = lax.dot_general(left, tiles_ref[k], (((1,), (1,)), ((), ())), preferred_element_type=F32)
                products.append((r, value))
            else:
                value = jnp.dot(source[r], tiles_ref[k], preferred_element_type=F32)
                products.append((c, value))
        for target, value in products:
            acc[target] += value
        return 0

    lax.fori_loop(0, CHUNK // UNROLL, body, 0)


def forward_kernel(coords, info, omega_ref, tiles_ref, keep_ref, give_ref, acc, sem):
    step = pl.program_id(0)
    half = acc.shape[0] // 2

    @pl.when(step == 0)
    def _():
        acc[...] = jnp.zeros_like(acc)

    @pl.when(step < live_chunks(info[0]))
    def _():
        sparse_step(True, coords, step * CHUNK, omega_ref, tiles_ref, acc)

    @pl.when(step == pl.num_programs(0) - 1)
    def _():
        core = info[1]
        one = pltpu.make_async_copy(acc.at[pl.ds(core * half, half)], keep_ref, sem.at[0])
        two = pltpu.make_async_copy(acc.at[pl.ds((1 - core) * half, half)], give_ref, sem.at[1])
        one.start()
        two.start()
        one.wait()
        two.wait()


def forward(tiles, coords, info, omega, blk_row):
    slots = tiles.shape[0]
    width = omega.shape[0]
    half = jax.ShapeDtypeStruct((blk_row // 2, width, TILE), F32)
    last = lambda i, coords, info: (jnp.minimum(i, live_chunks(info[0]) - 1), 0, 0)
    return pl.pallas_call(
        forward_kernel,
        out_shape=(half, half),
        grid_spec=pltpu.PrefetchScalarGridSpec(
            num_scalar_prefetch=2,
            grid=(slots // CHUNK,),
            in_specs=[
                pl.BlockSpec(omega.shape, lambda i, coords, info: (0, 0)),
                pl.BlockSpec((CHUNK, TILE, TILE), last),
            ],
            out_specs=[pl.BlockSpec(memory_space=pl.ANY)] * 2,
            scratch_shapes=[
                pltpu.VMEM((blk_row, width, TILE), F32),
                pltpu.SemaphoreType.DMA((2,)),
            ],
        ),
        compiler_params=params(),
        name="forward",
    )(coords, info, omega, tiles)


def pair_kernel(keep_ref, got_ref, out_ref, steps):
    count = keep_ref.shape[0]
    width = keep_ref.shape[1]

    def body(j, _):
        put_block(keep_ref[j] + got_ref[j], 0, j, out_ref, steps)
        return 0

    lax.fori_loop(0, count, body, 0)
    out_ref[0, count * width :, :] = steps[0].astype(jnp.int32).astype(I16)


def pair(keep, got, pieces):
    blocks, width, _ = keep.shape
    each = blocks // pieces
    rows = each * width + each
    return pl.pallas_call(
        pair_kernel,
        out_shape=jax.ShapeDtypeStruct((pieces, rows, TILE), I16),
        grid=(pieces,),
        in_specs=[pl.BlockSpec((each, width, TILE), lambda i: (i, 0, 0))] * 2,
        out_specs=pl.BlockSpec((1, rows, TILE), lambda i: (i, 0, 0)),
        scratch_shapes=[pltpu.VMEM((1, each, TILE), F32)],
        compiler_params=params(),
        name="pair",
    )(keep, got)


def gather_sum(in_ref, scale, j, width):
    total = None
    for s in range(in_ref.shape[0]):
        part = in_ref[s, pl.ds(pl.multiple_of(j * width, width), width), :].astype(jnp.int32).astype(F32)
        part = part * scale[s, pl.ds(j, 1), :]
        total = part if total is None else total + part
    return total


def scales(in_ref, scale, rows):
    for s in range(in_ref.shape[0]):
        scale[s] = factor(in_ref[s, rows:, :].astype(jnp.int32).astype(F32))


def share_kernel(in_ref, out_ref, scale):
    each, width, _ = out_ref.shape
    scales(in_ref, scale, each * width)

    def body(j, _):
        out_ref[j] = gather_sum(in_ref, scale, j, width).astype(out_ref.dtype)
        return 0

    lax.fori_loop(0, each, body, 0)


def share(parts, width):
    pieces, rows, _ = parts.shape
    each = rows // (width + 1)
    return pl.pallas_call(
        share_kernel,
        out_shape=jax.ShapeDtypeStruct((each, width, TILE), jnp.bfloat16),
        scratch_shapes=[pltpu.VMEM((pieces, each, TILE), F32)],
        compiler_params=params(),
        name="share",
    )(parts)


def backward_kernel(coords, info, mine_ref, theirs_ref, tiles_ref, out_ref, acc, inner, steps, sem):
    step = pl.program_id(0)
    half = inner.shape[0] // 2
    width = acc.shape[1]
    pieces = out_ref.shape[0]
    each = acc.shape[0] // pieces

    @pl.when(step == 0)
    def _():
        core = info[1]
        one = pltpu.make_async_copy(mine_ref, inner.at[pl.ds(core * half, half)], sem.at[0])
        two = pltpu.make_async_copy(theirs_ref, inner.at[pl.ds((1 - core) * half, half)], sem.at[1])
        one.start()
        two.start()
        acc[...] = jnp.zeros_like(acc)
        one.wait()
        two.wait()

    @pl.when(step < live_chunks(info[0]))
    def _():
        sparse_step(False, coords, step * CHUNK, inner, tiles_ref, acc)

    @pl.when(step == pl.num_programs(0) - 1)
    def _():
        def body(b, _):
            put_block(acc[b], lax.div(b, each), lax.rem(b, each), out_ref, steps)
            return 0

        lax.fori_loop(0, acc.shape[0], body, 0)
        for s in range(pieces):
            out_ref[s, each * width :, :] = steps[s].astype(jnp.int32).astype(I16)


def backward(tiles, coords, info, mine, theirs, blk_col, pieces):
    slots = tiles.shape[0]
    half, width, _ = mine.shape
    each = blk_col // pieces
    rows = each * width + each
    last = lambda i, coords, info: (jnp.minimum(i, live_chunks(info[0]) - 1), 0, 0)
    return pl.pallas_call(
        backward_kernel,
        out_shape=jax.ShapeDtypeStruct((pieces, rows, TILE), I16),
        grid_spec=pltpu.PrefetchScalarGridSpec(
            num_scalar_prefetch=2,
            grid=(slots // CHUNK,),
            in_specs=[
                pl.BlockSpec(memory_space=pl.ANY),
                pl.BlockSpec(memory_space=pl.ANY),
                pl.BlockSpec((CHUNK, TILE, TILE), last),
            ],
            out_specs=pl.BlockSpec((pieces, rows, TILE), lambda i, coords, info: (0, 0, 0)),
            scratch_shapes=[
                pltpu.VMEM((blk_col, width, TILE), F32),
                pltpu.VMEM((2 * half, width, TILE), jnp.bfloat16),
                pltpu.VMEM((pieces, each, TILE), F32),
                pltpu.SemaphoreType.DMA((2,)),
            ],
        ),
        compiler_params=params(),
        name="backward",
    )(coords, info, mine, theirs, tiles)


def again_kernel(in_ref, out_ref, scale, steps):
    each = scale.shape[1]
    width = (out_ref.shape[1] - each) // each
    scales(in_ref, scale, each * width)

    def body(j, _):
        put_block(gather_sum(in_ref, scale, j, width), 0, j, out_ref, steps)
        return 0

    lax.fori_loop(0, each, body, 0)
    out_ref[0, each * width :, :] = steps[0].astype(jnp.int32).astype(I16)


def again(parts, width):
    pieces, rows, _ = parts.shape
    each = rows // (width + 1)
    return pl.pallas_call(
        again_kernel,
        out_shape=jax.ShapeDtypeStruct((1, rows, TILE), I16),
        scratch_shapes=[pltpu.VMEM((pieces, each, TILE), F32), pltpu.VMEM((1, each, TILE), F32)],
        compiler_params=params(),
        name="again",
    )(parts)


def spread_kernel(in_ref, out_ref, scale):
    each = scale.shape[1]
    width = out_ref.shape[0]
    scales(in_ref, scale, each * width)
    for j in range(each):
        part = in_ref[0, j * width : (j + 1) * width, :].astype(jnp.int32).astype(F32)
        out_ref[:, j * TILE : (j + 1) * TILE] = part * scale[0, j : j + 1, :]


def spread(parts, width):
    pieces, rows, _ = parts.shape
    each = rows // (width + 1)
    return pl.pallas_call(
        spread_kernel,
        out_shape=jax.ShapeDtypeStruct((width, pieces * each * TILE), F32),
        grid=(pieces,),
        in_specs=[pl.BlockSpec((1, rows, TILE), lambda i: (i, 0, 0))],
        out_specs=pl.BlockSpec((width, each * TILE), lambda i: (0, i)),
        scratch_shapes=[pltpu.VMEM((1, each, TILE), F32)],
        compiler_params=params(),
        name="spread",
    )(parts)


def to_all(value, axes):
    count = lax.axis_size(axes)
    copies = jnp.broadcast_to(value[None], (count,) + value.shape)
    return lax.all_to_all(copies, axes, 0, 0, tiled=True)


def shards(tiles, tile_coords, tile_counts, omega):
    blocks = tiles[0, 0]
    coords = tile_coords[0, 0].reshape(-1)
    core = lax.axis_index("core")
    info = jnp.stack([tile_counts[0, 0], core.astype(jnp.int32)])
    width = omega.shape[0]
    blk_col = omega.shape[1] // TILE
    rows = lax.axis_size(ROW)
    chips = lax.axis_size(CHIPS)
    blk_row = blk_col * 2 * chips // rows
    swap = [(0, 1), (1, 0)]
    keep, give = forward(blocks, coords, info, omega, blk_row)
    got = lax.ppermute(give, "core", swap)
    parts = lax.all_to_all(pair(keep, got, chips), CHIPS, 0, 0, tiled=True)
    mine = to_all(share(parts, width), CHIPS).reshape(blk_row // 2, width, TILE)
    theirs = lax.ppermute(mine, "core", swap)
    out = backward(blocks, coords, info, mine, theirs, blk_col, rows)
    parts = lax.all_to_all(out, ROW, 0, 0, tiled=True)
    parts = to_all(again(parts, width)[0], ROW)
    return spread(parts, width)


def solution(mesh):
    fine = Mesh(mesh.devices.reshape(2, 4, 4, 2, 2), ("yh", "z", "x", "yl", "core"))
    col = ("x", "yl", "core")
    return jax.shard_map(
        shards,
        mesh=fine,
        in_specs=(
            P(ROW, col, None, None, None),
            P(ROW, col, None, None),
            P(ROW, col),
            P(None, col),
        ),
        out_specs=P(None, col),
        check_vma=False,
    )
```

```python
import functools

import jax
import jax.numpy as jnp
from jax import lax
from jax.experimental import pallas as pl
from jax.experimental.pallas import tpu as pltpu
from jax.sharding import Mesh
from jax.sharding import PartitionSpec as P

TILE = 128
CHUNK = 64
UNROLL = 64
LAG = 8
BLOCKS = 4
LEVEL = 32700.0
STEPS = 8.0
MIB = 1024 * 1024
ROW = ("yh", "z")
CHIPS = ("x", "yl")
F32 = jnp.float32
I16 = jnp.int16


def params(mib):
    return pltpu.CompilerParams(vmem_limit_bytes=mib * MIB)


def code(block):
    top = jnp.maximum(jnp.max(jnp.abs(block), axis=0, keepdims=True), 1e-30)
    step = jnp.ceil(jnp.log2(top) * STEPS)
    return step, jnp.exp2(step * (-1.0 / STEPS)) * LEVEL


def factor(step):
    return jnp.exp2(step * (1.0 / STEPS)) * (1.0 / LEVEL)


def put_blocks(read, count, piece, out_ref, steps):
    rows = out_ref.shape[1] - count
    width = rows // count

    def body(i, _):
        for u in range(BLOCKS):
            j = i * BLOCKS + u
            block = read(j)
            step, gain = code(block)
            whole = jnp.round(block * gain).astype(jnp.int32)
            out_ref[piece, pl.ds(pl.multiple_of(j * width, width), width), :] = whole.astype(I16)
            steps[pl.ds(j, 1), :] = step
        return 0

    lax.fori_loop(0, count // BLOCKS, body, 0)
    out_ref[piece, rows:, :] = steps[:count].astype(jnp.int32).astype(I16)


def sparse_step(transposed, coords, base, source, tiles_ref, acc):
    def body(i, _):
        waiting = []
        for u in range(UNROLL + LAG):
            if u < UNROLL:
                slot = base + i * UNROLL + u
                r, c = coords[2 * slot], coords[2 * slot + 1]
                if transposed:
                    left = source[:, pl.ds(pl.multiple_of(c * TILE, TILE), TILE)]
                    dims = (((1,), (1,)), ((), ()))
                    value = lax.dot_general(left, tiles_ref[slot], dims, preferred_element_type=F32)
                    waiting.append((r, value))
                else:
                    value = jnp.dot(source[r], tiles_ref[slot], preferred_element_type=F32)
                    waiting.append((c, value))
            if u >= LAG:
                target, value = waiting[u - LAG]
                acc[target] += value
        return 0

    lax.fori_loop(0, CHUNK // UNROLL, body, 0)


def fetch(count, tiles_ref, tiles, sem):
    def part(j):
        rows = pl.ds(j * CHUNK, CHUNK)
        return pltpu.make_async_copy(tiles_ref.at[rows], tiles.at[rows], sem.at[j])

    chunks = lax.div(count + (CHUNK - 1), CHUNK)
    lax.fori_loop(0, chunks, lambda j, _: (part(j).start(), 0)[1], 0)
    return chunks, part


def forward_kernel(coords, info, omega_ref, tiles_ref, keep_ref, give_ref, acc, omega, tiles, steps, tile_sem, sem):
    half = acc.shape[0] // 2
    width = acc.shape[1]
    load = pltpu.make_async_copy(omega_ref, omega, sem.at[0])
    load.start()
    chunks, part = fetch(info[0], tiles_ref, tiles, tile_sem)
    acc[...] = jnp.zeros_like(acc)
    load.wait()

    def chunk(j, _):
        part(j).wait()
        sparse_step(True, coords, j * CHUNK, omega, tiles, acc)
        return 0

    lax.fori_loop(0, chunks, chunk, 0)
    core = info[1]
    keep = pltpu.make_async_copy(acc.at[pl.ds(core * half, half)], keep_ref, sem.at[1])
    keep.start()
    put_blocks(lambda j: acc[(1 - core) * half + j], half, 0, give_ref, steps)
    keep.wait()


def forward(tiles, coords, info, omega, blk_row):
    slots = tiles.shape[0]
    width = omega.shape[0]
    half = blk_row // 2
    give = jax.ShapeDtypeStruct((1, half * (width + 1), TILE), I16)
    return pl.pallas_call(
        forward_kernel,
        out_shape=(jax.ShapeDtypeStruct((half, width, TILE), F32), give),
        in_specs=[pl.BlockSpec(memory_space=pltpu.SMEM)] * 2 + [pl.BlockSpec(memory_space=pl.ANY)] * 2,
        out_specs=[pl.BlockSpec(memory_space=pl.ANY), pl.BlockSpec(memory_space=pltpu.VMEM)],
        scratch_shapes=[
            pltpu.VMEM((blk_row, width, TILE), F32),
            pltpu.VMEM(omega.shape, omega.dtype),
            pltpu.VMEM(tiles.shape, tiles.dtype),
            pltpu.VMEM((half, TILE), F32),
            pltpu.SemaphoreType.DMA((slots // CHUNK,)),
            pltpu.SemaphoreType.DMA((2,)),
        ],
        compiler_params=params(40),
        name="forward",
    )(coords, info, omega, tiles)


def pair_kernel(keep_ref, got_ref, codes_ref, out_ref, scale, steps):
    each, width, _ = keep_ref.shape
    scale[...] = factor(codes_ref[0].astype(jnp.int32).astype(F32))

    def read(j):
        got = got_ref[0, pl.ds(pl.multiple_of(j * width, width), width), :].astype(jnp.int32).astype(F32)
        return keep_ref[j] + got * scale[pl.ds(j, 1), :]

    put_blocks(read, each, 0, out_ref, steps)


def pair(keep, got, pieces):
    blocks, width, _ = keep.shape
    each = blocks // pieces
    rows = each * width + each
    return pl.pallas_call(
        pair_kernel,
        out_shape=jax.ShapeDtypeStruct((pieces, rows, TILE), I16),
        grid=(pieces,),
        in_specs=[
            pl.BlockSpec((each, width, TILE), lambda i: (i, 0, 0)),
            pl.BlockSpec((1, each * width, TILE), lambda i: (0, i, 0)),
            pl.BlockSpec((1, each, TILE), lambda i: (0, pieces * width + i, 0)),
        ],
        out_specs=pl.BlockSpec((1, rows, TILE), lambda i: (i, 0, 0)),
        scratch_shapes=[pltpu.VMEM((each, TILE), F32)] * 2,
        compiler_params=params(12),
        name="pair",
    )(keep, got, got)


def gather_sum(in_ref, scale, j, width):
    total = None
    for s in range(in_ref.shape[0]):
        part = in_ref[s, pl.ds(pl.multiple_of(j * width, width), width), :].astype(jnp.int32).astype(F32)
        part = part * scale[s, pl.ds(j, 1), :]
        total = part if total is None else total + part
    return total


def scales(in_ref, scale, rows):
    for s in range(in_ref.shape[0]):
        scale[s] = factor(in_ref[s, rows:, :].astype(jnp.int32).astype(F32))


def share_kernel(in_ref, out_ref, scale):
    each, width, _ = out_ref.shape
    scales(in_ref, scale, each * width)

    def body(j, _):
        out_ref[j] = gather_sum(in_ref, scale, j, width).astype(out_ref.dtype)
        return 0

    lax.fori_loop(0, each, body, 0)


def share(parts, width):
    pieces, rows, _ = parts.shape
    each = rows // (width + 1)
    return pl.pallas_call(
        share_kernel,
        out_shape=jax.ShapeDtypeStruct((each, width, TILE), jnp.bfloat16),
        scratch_shapes=[pltpu.VMEM((pieces, each, TILE), F32)],
        compiler_params=params(12),
        name="share",
    )(parts)


def backward_kernel(coords, info, *refs):
    shares, (tiles_ref, out_ref, acc, inner, tiles, steps, tile_sem, sem) = refs[:-8], refs[-8:]
    pieces = out_ref.shape[0]
    each = acc.shape[0] // pieces
    size = shares[0].shape[0]
    loads = []
    for n, ref in enumerate(shares):
        to = inner.at[pl.ds(info[1 + n] * size, size)]
        loads.append(pltpu.make_async_copy(ref, to, sem.at[n]))
        loads[-1].start()
    chunks, part = fetch(info[0], tiles_ref, tiles, tile_sem)
    acc[...] = jnp.zeros_like(acc)
    for load in loads:
        load.wait()

    def chunk(j, _):
        part(j).wait()
        sparse_step(False, coords, j * CHUNK, inner, tiles, acc)
        return 0

    lax.fori_loop(0, chunks, chunk, 0)
    for s in range(pieces):
        put_blocks(lambda j: acc[s * each + j], each, s, out_ref, steps)


def backward(tiles, coords, info, shares, blk_col, pieces):
    slots = tiles.shape[0]
    size, width, _ = shares[0].shape
    each = blk_col // pieces
    rows = each * width + each
    return pl.pallas_call(
        backward_kernel,
        out_shape=jax.ShapeDtypeStruct((pieces, rows, TILE), I16),
        in_specs=[pl.BlockSpec(memory_space=pltpu.SMEM)] * 2 + [pl.BlockSpec(memory_space=pl.ANY)] * (len(shares) + 1),
        out_specs=pl.BlockSpec(memory_space=pltpu.VMEM),
        scratch_shapes=[
            pltpu.VMEM((blk_col, width, TILE), F32),
            pltpu.VMEM((len(shares) * size, width, TILE), jnp.bfloat16),
            pltpu.VMEM(tiles.shape, tiles.dtype),
            pltpu.VMEM((each, TILE), F32),
            pltpu.SemaphoreType.DMA((slots // CHUNK,)),
            pltpu.SemaphoreType.DMA((len(shares),)),
        ],
        compiler_params=params(40),
        name="backward",
    )(coords, info, *shares, tiles)


def again_kernel(in_ref, out_ref, scale, steps):
    each = scale.shape[1]
    width = (out_ref.shape[1] - each) // each
    scales(in_ref, scale, each * width)
    put_blocks(lambda j: gather_sum(in_ref, scale, j, width), each, 0, out_ref, steps)


def again(parts, width):
    pieces, rows, _ = parts.shape
    each = rows // (width + 1)
    return pl.pallas_call(
        again_kernel,
        out_shape=jax.ShapeDtypeStruct((1, rows, TILE), I16),
        scratch_shapes=[pltpu.VMEM((pieces, each, TILE), F32), pltpu.VMEM((each, TILE), F32)],
        compiler_params=params(12),
        name="again",
    )(parts)


def spread_kernel(info, *refs):
    parts, (out_ref, scale, buffer, sem) = refs[:-4], refs[-4:]
    each = scale.shape[0]
    width = buffer.shape[1]
    size = each * TILE

    def store(n):
        columns = pl.ds(pl.multiple_of(info[n] * size, size), size)
        return pltpu.make_async_copy(buffer.at[n], out_ref.at[:, columns], sem.at[n])

    for n, ref in enumerate(parts):
        scale[...] = factor(ref[each * width :, :].astype(jnp.int32).astype(F32))
        for j in range(each):
            part = ref[j * width : (j + 1) * width, :].astype(jnp.int32).astype(F32)
            buffer[n, :, j * TILE : (j + 1) * TILE] = part * scale[j : j + 1, :]
        store(n).start()
    for n in range(len(parts)):
        store(n).wait()


def spread(info, parts, width):
    rows = parts[0].shape[0]
    each = rows // (width + 1)
    count = len(parts)
    return pl.pallas_call(
        spread_kernel,
        out_shape=jax.ShapeDtypeStruct((width, count * each * TILE), F32),
        in_specs=[pl.BlockSpec(memory_space=pltpu.SMEM)] + [pl.BlockSpec(memory_space=pltpu.VMEM)] * count,
        out_specs=pl.BlockSpec(memory_space=pl.ANY),
        scratch_shapes=[
            pltpu.VMEM((each, TILE), F32),
            pltpu.VMEM((count, width, each * TILE), F32),
            pltpu.SemaphoreType.DMA((count,)),
        ],
        compiler_params=params(16),
        name="spread",
    )(info, *parts)


def shift(value, axis, by):
    count = lax.axis_size(axis)
    return lax.ppermute(value, axis, [(i, (i + by) % count) for i in range(count)])


def gather(value, ring, pair):
    i, j = lax.axis_index(ring), lax.axis_index(pair)
    across = shift(value, pair, 1)
    up = shift(value, ring, 1)
    down = shift(value, ring, -1)
    down_across = shift(down, pair, 1)
    up_across = shift(across, ring, 1)
    far = shift(down, ring, -1)
    far_across = shift(far, pair, 1)
    shares = [value, across, up, down, up_across, down_across, far, far_across]
    hops = [(0, 0), (0, 1), (-1, 0), (1, 0), (-1, 1), (1, 1), (2, 0), (2, 1)]
    return shares, [lax.rem(i + a + 4, 4) * 2 + lax.rem(j + b, 2) for a, b in hops]


def shards(tiles, tile_coords, tile_counts, omega):
    blocks = tiles[0, 0]
    coords = tile_coords[0, 0].reshape(-1)
    count = tile_counts[0, 0]
    core = lax.axis_index("core")
    width = omega.shape[0]
    blk_col = omega.shape[1] // TILE
    rows = lax.axis_size(ROW)
    chips = lax.axis_size(CHIPS)
    blk_row = blk_col * 2 * chips // rows
    keep, give = forward(blocks, coords, jnp.stack([count, core]), omega, blk_row)
    parts = lax.all_to_all(pair(keep, shift(give, "core", 1), chips), CHIPS, 0, 0, tiled=True)
    mine, places = gather(share(parts, width), *CHIPS)
    theirs = [shift(value, "core", 1) for value in mine]
    places = [core * chips + p for p in places] + [(1 - core) * chips + p for p in places]
    out = backward(blocks, coords, jnp.stack([count, *places]), mine + theirs, blk_col, rows)
    parts = lax.all_to_all(out, ROW, 0, 0, tiled=True)
    parts, places = gather(again(parts, width)[0], "z", "yh")
    places = [lax.rem(p, 2) * 4 + lax.div(p, 2) for p in places]
    return spread(jnp.stack(places), parts, width)


def solution(mesh):
    fine = Mesh(mesh.devices.reshape(2, 4, 4, 2, 2), ("yh", "z", "x", "yl", "core"))
    col = ("x", "yl", "core")
    return jax.shard_map(
        shards,
        mesh=fine,
        in_specs=(
            P(ROW, col, None, None, None),
            P(ROW, col, None, None),
            P(ROW, col),
            P(None, col),
        ),
        out_specs=P(None, col),
        check_vma=False,
    )
```

```python
import functools

import jax
import jax.numpy as jnp
from jax import lax
from jax.experimental import pallas as pl
from jax.experimental.pallas import tpu as pltpu
from jax.sharding import Mesh
from jax.sharding import PartitionSpec as P

TILE = 128
CHUNK = 64
UNROLL = 64
LAG = 8
BLOCKS = 32
LEVEL = 32700.0
STEPS = 8.0
MIB = 1024 * 1024
ROW = ("yh", "z")
CHIPS = ("x", "yl")
HOPS = [(0, 0), (0, 1), (-1, 0), (1, 0), (-1, 1), (1, 1), (2, 0), (2, 1)]
SENT = (2, 4, 5, 7)
KEPT = (0, 1, 3, 6)
EARLY = (0, 1, 2, 3)
LATE = (4, 5, 6, 7)
PLACES = 2
LINES = PLACES + len(HOPS)
F32 = jnp.float32
I16 = jnp.int16


def params(mib):
    return pltpu.CompilerParams(vmem_limit_bytes=mib * MIB)


def code(block):
    top = jnp.maximum(jnp.max(jnp.abs(block), axis=0, keepdims=True), 1e-30)
    step = jnp.ceil(jnp.log2(top) * STEPS)
    return step, jnp.exp2(step * (-1.0 / STEPS)) * LEVEL


def factor(step):
    return jnp.exp2(step * (1.0 / STEPS)) * (1.0 / LEVEL)


def put_blocks(read, count, out_ref, steps):
    rows = out_ref.shape[0] - count
    width = rows // count
    unroll = min(BLOCKS, count)

    def body(i, _):
        for u in range(unroll):
            j = i * unroll + u
            block = read(j)
            step, gain = code(block)
            whole = jnp.round(block * gain).astype(jnp.int32)
            out_ref[pl.ds(pl.multiple_of(j * width, width), width), :] = whole.astype(I16)
            steps[pl.ds(j, 1), :] = step
        return 0

    lax.fori_loop(0, count // unroll, body, 0)
    out_ref[rows:, :] = steps[:count].astype(jnp.int32).astype(I16)


def sparse_step(transposed, coords, base, source, tiles_ref, acc):
    def body(i, _):
        waiting = []
        for u in range(UNROLL + LAG):
            if u < UNROLL:
                slot = base + i * UNROLL + u
                r, c = coords[0, slot], coords[1, slot]
                if transposed:
                    left = source[:, pl.ds(pl.multiple_of(c * TILE, TILE), TILE)]
                    dims = (((1,), (1,)), ((), ()))
                    value = lax.dot_general(tiles_ref[slot], left, dims, preferred_element_type=F32)
                    waiting.append((r, value))
                else:
                    value = jnp.dot(source[r], tiles_ref[slot], preferred_element_type=F32)
                    waiting.append((c, value))
            if u >= LAG:
                target, value = waiting[u - LAG]
                acc[target] += value
        return 0

    lax.fori_loop(0, CHUNK // UNROLL, body, 0)


def fetch(count, tiles_ref, tiles, sem):
    def part(j):
        rows = pl.ds(j * CHUNK, CHUNK)
        return pltpu.make_async_copy(tiles_ref.at[rows], tiles.at[rows], sem.at[j])

    chunks = lax.div(count + (CHUNK - 1), CHUNK)
    lax.fori_loop(0, chunks, lambda j, _: (part(j).start(), 0)[1], 0)
    return chunks, part


def forward_kernel(coords, info, omega_ref, tiles_ref, keep_ref, give_ref, acc, omega, tiles, coded, steps, tile_sem, sem):
    half = acc.shape[0] // 2
    load = pltpu.make_async_copy(omega_ref, omega, sem.at[0])
    load.start()
    chunks, part = fetch(info[0], tiles_ref, tiles, tile_sem)
    acc[...] = jnp.zeros_like(acc)
    load.wait()

    def chunk(j, _):
        part(j).wait()
        sparse_step(True, coords, j * CHUNK, omega, tiles, acc)
        return 0

    lax.fori_loop(0, chunks, chunk, 0)
    core = info[1]
    stores = []
    for n, (out_ref, first) in enumerate(((give_ref, (1 - core) * half), (keep_ref, core * half))):
        put_blocks(lambda j: acc[first + j].T, half, coded.at[n], steps)
        stores.append(pltpu.make_async_copy(coded.at[n], out_ref, sem.at[1 + n]))
        stores[-1].start()
    for store in stores:
        store.wait()


def forward(tiles, coords, info, omega, blk_row):
    slots = tiles.shape[0]
    width = omega.shape[0]
    half = blk_row // 2
    coded = jax.ShapeDtypeStruct((half * (width + 1), TILE), I16)
    return pl.pallas_call(
        forward_kernel,
        out_shape=(coded, coded),
        in_specs=[pl.BlockSpec(memory_space=pltpu.SMEM)] * 2 + [pl.BlockSpec(memory_space=pltpu.HBM)] * 2,
        out_specs=[pl.BlockSpec(memory_space=pltpu.HBM)] * 2,
        scratch_shapes=[
            pltpu.VMEM((blk_row, TILE, width), F32),
            pltpu.VMEM(omega.shape, omega.dtype),
            pltpu.VMEM(tiles.shape, tiles.dtype),
            pltpu.VMEM((2, *coded.shape), I16),
            pltpu.VMEM((half, TILE), F32),
            pltpu.SemaphoreType.DMA((slots // CHUNK,)),
            pltpu.SemaphoreType.DMA((3,)),
        ],
        compiler_params=params(60),
        name="forward",
    )(coords, info, omega, tiles)


def plain_kernel(in_ref, out_ref, scale):
    blocks, width, _ = out_ref.shape
    scales((in_ref,), scale, blocks * width)

    def body(j, _):
        part = in_ref[pl.ds(pl.multiple_of(j * width, width), width), :].astype(jnp.int32).astype(F32)
        out_ref[j] = part * scale[0, pl.ds(j, 1), :]
        return 0

    lax.fori_loop(0, blocks, body, 0, unroll=8)


def plain(coded, width):
    blocks = coded.shape[0] // (width + 1)
    return pl.pallas_call(
        plain_kernel,
        out_shape=jax.ShapeDtypeStruct((blocks, width, TILE), F32),
        in_specs=[pl.BlockSpec(memory_space=pltpu.VMEM)],
        out_specs=pl.BlockSpec(memory_space=pltpu.VMEM),
        scratch_shapes=[pltpu.VMEM((1, blocks, TILE), F32)],
        compiler_params=params(14),
        name="plain",
    )(coded)


def pair_kernel(which, sent, info, keep_ref, got_ref, *refs):
    outs, (scale, steps) = refs[:-2], refs[-2:]
    blocks, width, _ = keep_ref.shape
    each = blocks // len(HOPS)
    scales((got_ref,), scale, blocks * width)
    for n, out_ref in zip(which, outs):
        first = info[PLACES + n] * each

        def read(j):
            b = first + j
            got = got_ref[pl.ds(pl.multiple_of(b * width, width), width), :].astype(jnp.int32).astype(F32)
            return keep_ref[b] + got * scale[0, pl.ds(b, 1), :]

        if sent:
            put_blocks(read, each, out_ref, steps)
        else:

            def body(j, _):
                out_ref[j] = read(j)
                return 0

            lax.fori_loop(0, each, body, 0, unroll=8)


def pair(info, keep, got, which, sent):
    blocks, width, _ = keep.shape
    each = blocks // len(HOPS)
    coded = jax.ShapeDtypeStruct((each * width + each, TILE), I16)
    return pl.pallas_call(
        functools.partial(pair_kernel, which, sent),
        out_shape=[coded if sent else jax.ShapeDtypeStruct((each, width, TILE), F32)] * len(which),
        in_specs=[pl.BlockSpec(memory_space=s) for s in (pltpu.SMEM, pltpu.VMEM, pltpu.VMEM)],
        out_specs=[pl.BlockSpec(memory_space=pltpu.VMEM)] * len(which),
        scratch_shapes=[pltpu.VMEM((1, blocks, TILE), F32), pltpu.VMEM((each, TILE), F32)],
        compiler_params=params(14),
        name="pair",
    )(info, keep, got)


def scales(parts, scale, rows):
    for n, ref in enumerate(parts):
        scale[n] = factor(ref[rows:, :].astype(jnp.int32).astype(F32))


def gather_sum(own_ref, parts, scale, j, width):
    total = own_ref[j]
    for n, ref in enumerate(parts):
        part = ref[pl.ds(pl.multiple_of(j * width, width), width), :].astype(jnp.int32).astype(F32)
        total = total + part * scale[n, pl.ds(j, 1), :]
    return total


def share_kernel(own_ref, *refs):
    parts, (out_ref, scale) = refs[:-2], refs[-2:]
    each, width, _ = own_ref.shape
    scales(parts, scale, each * width)

    def body(j, _):
        out_ref[j] = gather_sum(own_ref, parts, scale, j, width).astype(out_ref.dtype)
        return 0

    lax.fori_loop(0, each, body, 0, unroll=8)


def share(own, parts):
    each = own.shape[0]
    return pl.pallas_call(
        share_kernel,
        out_shape=jax.ShapeDtypeStruct(own.shape, jnp.bfloat16),
        scratch_shapes=[pltpu.VMEM((len(parts), each, TILE), F32)],
        compiler_params=params(12),
        name="share",
    )(own, *parts)


def merge_kernel(own_ref, *refs):
    parts, (out_ref, scale, steps) = refs[:-3], refs[-3:]
    each, width, _ = own_ref.shape
    scales(parts, scale, each * width)
    put_blocks(lambda j: gather_sum(own_ref, parts, scale, j, width), each, out_ref, steps)


def merge(own, parts):
    each = own.shape[0]
    return pl.pallas_call(
        merge_kernel,
        out_shape=jax.ShapeDtypeStruct(parts[0].shape, I16),
        scratch_shapes=[pltpu.VMEM((len(parts), each, TILE), F32), pltpu.VMEM((each, TILE), F32)],
        compiler_params=params(12),
        name="merge",
    )(own, *parts)


def backward_kernel(coords, info, *refs):
    acc, inner, tiles, steps, tile_sem, sem, out_sem = refs[-7:]
    count = inner.shape[0] // refs[0].shape[0]
    shares, tiles_ref, outs = refs[:count], refs[count], refs[count + 1 : -7]
    each = acc.shape[0] // len(outs)
    size = shares[0].shape[0]
    core = info[1]
    loads = []
    for n, ref in enumerate(shares):
        half = core if n < len(HOPS) else 1 - core
        place = half * len(HOPS) + info[PLACES + n % len(HOPS)]
        loads.append(pltpu.make_async_copy(ref, inner.at[pl.ds(place * size, size)], sem.at[n]))
        loads[-1].start()
    chunks, part = fetch(info[0], tiles_ref, tiles, tile_sem)
    acc[...] = jnp.zeros_like(acc)
    for load in loads:
        load.wait()

    def chunk(j, _):
        part(j).wait()
        sparse_step(False, coords, j * CHUNK, inner, tiles, acc)
        return 0

    lax.fori_loop(0, chunks, chunk, 0)
    stores = []
    for n, out_ref in zip(KEPT, outs[len(SENT) :]):
        first = info[LINES + n] * each
        stores.append(pltpu.make_async_copy(acc.at[pl.ds(first, each)], out_ref, out_sem.at[len(stores)]))
        stores[-1].start()
    for n, out_ref in zip(SENT, outs):
        first = info[LINES + n] * each
        put_blocks(lambda j: acc[first + j], each, out_ref, steps)
    for store in stores:
        store.wait()


def backward(tiles, coords, info, shares, blk_col):
    slots = tiles.shape[0]
    size, width, _ = shares[0].shape
    each = blk_col // len(HOPS)
    coded = jax.ShapeDtypeStruct((each * width + each, TILE), I16)
    plain = jax.ShapeDtypeStruct((each, width, TILE), F32)
    return pl.pallas_call(
        backward_kernel,
        out_shape=[coded] * len(SENT) + [plain] * len(KEPT),
        in_specs=[pl.BlockSpec(memory_space=pltpu.SMEM)] * 2 + [pl.BlockSpec(memory_space=pl.ANY)] * len(shares) + [pl.BlockSpec(memory_space=pltpu.HBM)],
        out_specs=[pl.BlockSpec(memory_space=pltpu.VMEM)] * len(SENT) + [pl.BlockSpec(memory_space=pl.ANY)] * len(KEPT),
        scratch_shapes=[
            pltpu.VMEM((blk_col, width, TILE), F32),
            pltpu.VMEM((len(shares) * size, width, TILE), jnp.bfloat16),
            pltpu.VMEM(tiles.shape, tiles.dtype),
            pltpu.VMEM((each, TILE), F32),
            pltpu.SemaphoreType.DMA((slots // CHUNK,)),
            pltpu.SemaphoreType.DMA((len(shares),)),
            pltpu.SemaphoreType.DMA((len(KEPT),)),
        ],
        compiler_params=params(40),
        name="backward",
    )(coords, info, *shares, tiles)


def spread_kernel(which, info, *refs):
    parts, (out_ref, scale, buffer, sem) = refs[: len(which)], refs[-4:]
    each = scale.shape[0]
    width = buffer.shape[1]
    size = each * TILE
    stores = []
    for k, (n, ref) in enumerate(zip(which, parts)):
        scale[...] = factor(ref[each * width :, :].astype(jnp.int32).astype(F32))
        for j in range(each):
            part = ref[j * width : (j + 1) * width, :].astype(jnp.int32).astype(F32)
            buffer[k, :, j * TILE : (j + 1) * TILE] = part * scale[j : j + 1, :]
        columns = pl.ds(pl.multiple_of(info[LINES + n] * size, size), size)
        stores.append(pltpu.make_async_copy(buffer.at[k], out_ref.at[:, columns], sem.at[k]))
        stores[-1].start()
    for store in stores:
        store.wait()


def spread(info, parts, width, which, out=None):
    rows = parts[0].shape[0]
    each = rows // (width + 1)
    vmem, hbm = pl.BlockSpec(memory_space=pltpu.VMEM), pl.BlockSpec(memory_space=pl.ANY)
    given = [] if out is None else [out]
    return pl.pallas_call(
        functools.partial(spread_kernel, which),
        out_shape=jax.ShapeDtypeStruct((width, len(HOPS) * each * TILE), F32),
        in_specs=[pl.BlockSpec(memory_space=pltpu.SMEM)] + [vmem] * len(which) + [hbm] * len(given),
        out_specs=hbm,
        scratch_shapes=[
            pltpu.VMEM((each, TILE), F32),
            pltpu.VMEM((len(which), width, each * TILE), F32),
            pltpu.SemaphoreType.DMA((len(which),)),
        ],
        input_output_aliases={1 + len(which): 0} if given else {},
        compiler_params=params(16),
        name="spread",
    )(info, *[parts[n] for n in which], *given)


def shift(value, axis, by):
    count = lax.axis_size(axis)
    return lax.ppermute(value, axis, [(i, (i + by) % count) for i in range(count)])


def gather(value, ring, pair, direct):
    across = shift(value, pair, 1)
    up = shift(value, ring, 1)
    down = shift(value, ring, -1)
    down_across = shift(down, pair, 1)
    up_across = shift(across, ring, 1)
    far = shift(value, ring, 2) if direct else shift(down, ring, -1)
    far_across = shift(far, pair, 1)
    return [value, across, up, down, up_across, down_across, far, far_across]


def numbers(ring, pair):
    i, j = lax.axis_index(ring), lax.axis_index(pair)
    return [lax.rem(i + a + 4, 4) * 2 + lax.rem(j + b, 2) for a, b in HOPS]


def scatter(sent, kept, ring, pair, last):
    down, down_across, up_across, far_across = sent
    own, across, up, far = kept
    far_across = shift(far_across, pair, 1)
    up_across = shift(up_across, pair, 1)
    down_across = shift(down_across, ring, -1)
    down = shift(down, ring, -1)
    far = shift(merge(far, [far_across]), ring, 2)
    up = shift(merge(up, [up_across]), ring, 1)
    across = shift(merge(across, [down_across]), pair, 1)
    return last(own, [down, across, up, far])


def shards(tiles, tile_coords, tile_counts, omega):
    blocks = tiles[0, 0]
    coords = tile_coords[0, 0].T
    core = lax.axis_index("core")
    width = omega.shape[0]
    blk_col = omega.shape[1] // TILE
    rows = lax.axis_size(ROW)
    chips = lax.axis_size(CHIPS)
    blk_row = blk_col * 2 * chips // rows
    lines = [lax.rem(p, 2) * 4 + lax.div(p, 2) for p in numbers("z", "yh")]
    info = jnp.stack([tile_counts[0, 0], core, *numbers(*CHIPS), *lines])
    keep, give = forward(blocks, coords, info, omega, blk_row)
    got = shift(give, "core", 1)
    keep = plain(keep, width)
    sent = pair(info, keep, got, SENT, True)
    kept = pair(info, keep, got, KEPT, False)
    mine = gather(scatter(sent, kept, *CHIPS, share), *CHIPS, False)
    theirs = [shift(value, "core", 1) for value in mine]
    out = backward(blocks, coords, info, mine + theirs, blk_col)
    parts = gather(scatter(out[: len(SENT)], out[len(SENT) :], "z", "yh", merge), "z", "yh", True)
    return spread(info, parts, width, LATE, spread(info, parts, width, EARLY))


def solution(mesh):
    fine = Mesh(mesh.devices.reshape(2, 4, 4, 2, 2), ("yh", "z", "x", "yl", "core"))
    col = ("x", "yl", "core")
    return jax.shard_map(
        shards,
        mesh=fine,
        in_specs=(
            P(ROW, col, None, None, None),
            P(ROW, col, None, None),
            P(ROW, col),
            P(None, col),
        ),
        out_specs=P(None, col),
        check_vma=False,
    )
```

```python
import functools

import jax
import jax.numpy as jnp
from jax import lax
from jax.experimental import pallas as pl
from jax.experimental.pallas import tpu as pltpu
from jax.sharding import Mesh
from jax.sharding import PartitionSpec as P

TILE = 128
CHUNK = 64
UNROLL = 64
LAG = 8
BLOCKS = 32
LEVEL = 32700.0
STEPS = 8.0
MIB = 1024 * 1024
ROW = ("yh", "z")
CHIPS = ("x", "yl")
HOPS = [(0, 0), (0, 1), (-1, 0), (1, 0), (-1, 1), (1, 1), (2, 0), (2, 1)]
SENT = (7, 5, 4, 3, 2)
KEPT = (0, 1, 6)
FIRST = 3
EARLY = (0, 1, 2, 3)
LATE = (4, 5, 6, 7)
PLACES = 2
LINES = PLACES + len(HOPS)
F32 = jnp.float32
I16 = jnp.int16


def params(mib):
    return pltpu.CompilerParams(vmem_limit_bytes=mib * MIB)


def code(block):
    top = jnp.maximum(jnp.max(jnp.abs(block), axis=0, keepdims=True), 1e-30)
    step = jnp.ceil(jnp.log2(top) * STEPS)
    return step, jnp.exp2(step * (-1.0 / STEPS)) * LEVEL


def factor(step):
    return jnp.exp2(step * (1.0 / STEPS)) * (1.0 / LEVEL)


def put_blocks(read, count, out_ref, steps):
    rows = out_ref.shape[0] - count
    width = rows // count
    unroll = min(BLOCKS, count)

    def body(i, _):
        for u in range(unroll):
            j = i * unroll + u
            block = read(j)
            step, gain = code(block)
            whole = jnp.round(block * gain).astype(jnp.int32)
            out_ref[pl.ds(pl.multiple_of(j * width, width), width), :] = whole.astype(I16)
            steps[pl.ds(j, 1), :] = step
        return 0

    lax.fori_loop(0, count // unroll, body, 0)
    out_ref[rows:, :] = steps[:count].astype(jnp.int32).astype(I16)


def sparse_step(transposed, coords, base, source, tiles_ref, acc):
    def body(i, _):
        waiting = []
        for u in range(UNROLL + LAG):
            if u < UNROLL:
                slot = base + i * UNROLL + u
                r, c = coords[0, slot], coords[1, slot]
                if transposed:
                    left = source[:, pl.ds(pl.multiple_of(c * TILE, TILE), TILE)]
                    dims = (((1,), (1,)), ((), ()))
                    value = lax.dot_general(tiles_ref[slot], left, dims, preferred_element_type=F32)
                    waiting.append((r, value))
                else:
                    value = jnp.dot(source[r], tiles_ref[slot], preferred_element_type=F32)
                    waiting.append((c, value))
            if u >= LAG:
                target, value = waiting[u - LAG]
                acc[target] += value
        return 0

    lax.fori_loop(0, CHUNK // UNROLL, body, 0)


def fetch(count, tiles_ref, tiles, sem):
    def part(j):
        rows = pl.ds(j * CHUNK, CHUNK)
        return pltpu.make_async_copy(tiles_ref.at[rows], tiles.at[rows], sem.at[j])

    chunks = lax.div(count + (CHUNK - 1), CHUNK)
    lax.fori_loop(0, chunks, lambda j, _: (part(j).start(), 0)[1], 0)
    return chunks, part


def forward_kernel(coords, info, omega_ref, tiles_ref, keep_ref, give_ref, acc, omega, tiles, coded, steps, tile_sem, sem):
    half = acc.shape[0] // 2
    load = pltpu.make_async_copy(omega_ref, omega, sem.at[0])
    load.start()
    chunks, part = fetch(info[0], tiles_ref, tiles, tile_sem)
    acc[...] = jnp.zeros_like(acc)
    load.wait()

    def chunk(j, _):
        part(j).wait()
        sparse_step(True, coords, j * CHUNK, omega, tiles, acc)
        return 0

    lax.fori_loop(0, chunks, chunk, 0)
    core = info[1]
    stores = []
    for n, (out_ref, first) in enumerate(((give_ref, (1 - core) * half), (keep_ref, core * half))):
        put_blocks(lambda j: acc[first + j].T, half, coded.at[n], steps)
        stores.append(pltpu.make_async_copy(coded.at[n], out_ref, sem.at[1 + n]))
        stores[-1].start()
    for store in stores:
        store.wait()


def forward(tiles, coords, info, omega, blk_row):
    slots = tiles.shape[0]
    width = omega.shape[0]
    half = blk_row // 2
    coded = jax.ShapeDtypeStruct((half * (width + 1), TILE), I16)
    return pl.pallas_call(
        forward_kernel,
        out_shape=(coded, coded),
        in_specs=[pl.BlockSpec(memory_space=pltpu.SMEM)] * 2 + [pl.BlockSpec(memory_space=pltpu.HBM)] * 2,
        out_specs=[pl.BlockSpec(memory_space=pltpu.HBM)] * 2,
        scratch_shapes=[
            pltpu.VMEM((blk_row, TILE, width), F32),
            pltpu.VMEM(omega.shape, omega.dtype),
            pltpu.VMEM(tiles.shape, tiles.dtype),
            pltpu.VMEM((2, *coded.shape), I16),
            pltpu.VMEM((half, TILE), F32),
            pltpu.SemaphoreType.DMA((slots // CHUNK,)),
            pltpu.SemaphoreType.DMA((3,)),
        ],
        compiler_params=params(60),
        name="forward",
    )(coords, info, omega, tiles)


def plain_kernel(in_ref, out_ref, scale):
    blocks, width, _ = out_ref.shape
    scales((in_ref,), scale, blocks * width)

    def body(j, _):
        part = in_ref[pl.ds(pl.multiple_of(j * width, width), width), :].astype(jnp.int32).astype(F32)
        out_ref[j] = part * scale[0, pl.ds(j, 1), :]
        return 0

    lax.fori_loop(0, blocks, body, 0, unroll=8)


def plain(coded, width):
    blocks = coded.shape[0] // (width + 1)
    return pl.pallas_call(
        plain_kernel,
        out_shape=jax.ShapeDtypeStruct((blocks, width, TILE), F32),
        in_specs=[pl.BlockSpec(memory_space=pltpu.VMEM)],
        out_specs=pl.BlockSpec(memory_space=pltpu.VMEM),
        scratch_shapes=[pltpu.VMEM((1, blocks, TILE), F32)],
        compiler_params=params(14),
        name="plain",
    )(coded)


def pair_kernel(which, sent, info, keep_ref, got_ref, *refs):
    outs, (scale, steps) = refs[:-2], refs[-2:]
    blocks, width, _ = keep_ref.shape
    each = blocks // len(HOPS)
    scales((got_ref,), scale, blocks * width)
    for k, (n, out_ref) in enumerate(zip(which, outs)):
        first = info[PLACES + n] * each

        def read(j):
            b = first + j
            got = got_ref[pl.ds(pl.multiple_of(b * width, width), width), :].astype(jnp.int32).astype(F32)
            return keep_ref[b] + got * scale[0, pl.ds(b, 1), :]

        if k < sent:
            put_blocks(read, each, out_ref, steps)
        else:

            def body(j, _):
                out_ref[j] = read(j)
                return 0

            lax.fori_loop(0, each, body, 0, unroll=8)


def pair(info, keep, got, which, sent):
    blocks, width, _ = keep.shape
    each = blocks // len(HOPS)
    coded = jax.ShapeDtypeStruct((each * width + each, TILE), I16)
    return pl.pallas_call(
        functools.partial(pair_kernel, which, sent),
        out_shape=[coded] * sent + [jax.ShapeDtypeStruct((each, width, TILE), F32)] * (len(which) - sent),
        in_specs=[pl.BlockSpec(memory_space=s) for s in (pltpu.SMEM, pltpu.VMEM, pltpu.VMEM)],
        out_specs=[pl.BlockSpec(memory_space=pltpu.VMEM)] * len(which),
        scratch_shapes=[pltpu.VMEM((1, blocks, TILE), F32), pltpu.VMEM((each, TILE), F32)],
        compiler_params=params(14),
        name="pair",
    )(info, keep, got)


def scales(parts, scale, rows):
    for n, ref in enumerate(parts):
        scale[n] = factor(ref[rows:, :].astype(jnp.int32).astype(F32))


def gather_sum(own_ref, parts, scale, j, width):
    total = own_ref[j]
    for n, ref in enumerate(parts):
        part = ref[pl.ds(pl.multiple_of(j * width, width), width), :].astype(jnp.int32).astype(F32)
        total = total + part * scale[n, pl.ds(j, 1), :]
    return total


def share_kernel(own_ref, *refs):
    parts, (out_ref, scale) = refs[:-2], refs[-2:]
    each, width, _ = own_ref.shape
    scales(parts, scale, each * width)

    def body(j, _):
        out_ref[j] = gather_sum(own_ref, parts, scale, j, width).astype(out_ref.dtype)
        return 0

    lax.fori_loop(0, each, body, 0, unroll=8)


def share(own, parts):
    each = own.shape[0]
    return pl.pallas_call(
        share_kernel,
        out_shape=jax.ShapeDtypeStruct(own.shape, jnp.bfloat16),
        scratch_shapes=[pltpu.VMEM((len(parts), each, TILE), F32)],
        compiler_params=params(12),
        name="share",
    )(own, *parts)


def merge_kernel(own_ref, *refs):
    parts, (out_ref, scale, steps) = refs[:-3], refs[-3:]
    each, width, _ = own_ref.shape
    scales(parts, scale, each * width)
    put_blocks(lambda j: gather_sum(own_ref, parts, scale, j, width), each, out_ref, steps)


def merge(own, parts):
    each = own.shape[0]
    return pl.pallas_call(
        merge_kernel,
        out_shape=jax.ShapeDtypeStruct(parts[0].shape, I16),
        scratch_shapes=[pltpu.VMEM((len(parts), each, TILE), F32), pltpu.VMEM((each, TILE), F32)],
        compiler_params=params(12),
        name="merge",
    )(own, *parts)


def backward_kernel(coords, info, *refs):
    acc, inner, tiles, steps, tile_sem, sem, out_sem = refs[-7:]
    count = inner.shape[0] // refs[0].shape[0]
    shares, tiles_ref, outs = refs[:count], refs[count], refs[count + 1 : -7]
    each = acc.shape[0] // len(outs)
    size = shares[0].shape[0]
    core = info[1]
    loads = []
    for n, ref in enumerate(shares):
        half = core if n < len(HOPS) else 1 - core
        place = half * len(HOPS) + info[PLACES + n % len(HOPS)]
        loads.append(pltpu.make_async_copy(ref, inner.at[pl.ds(place * size, size)], sem.at[n]))
        loads[-1].start()
    chunks, part = fetch(info[0], tiles_ref, tiles, tile_sem)
    acc[...] = jnp.zeros_like(acc)
    for load in loads:
        load.wait()

    def chunk(j, _):
        part(j).wait()
        sparse_step(False, coords, j * CHUNK, inner, tiles, acc)
        return 0

    lax.fori_loop(0, chunks, chunk, 0)
    stores = []
    for n, out_ref in zip(KEPT, outs[len(SENT) :]):
        first = info[LINES + n] * each
        stores.append(pltpu.make_async_copy(acc.at[pl.ds(first, each)], out_ref, out_sem.at[len(stores)]))
        stores[-1].start()
    for n, out_ref in zip(SENT, outs):
        first = info[LINES + n] * each
        put_blocks(lambda j: acc[first + j], each, out_ref, steps)
    for store in stores:
        store.wait()


def backward(tiles, coords, info, shares, blk_col):
    slots = tiles.shape[0]
    size, width, _ = shares[0].shape
    each = blk_col // len(HOPS)
    coded = jax.ShapeDtypeStruct((each * width + each, TILE), I16)
    plain = jax.ShapeDtypeStruct((each, width, TILE), F32)
    return pl.pallas_call(
        backward_kernel,
        out_shape=[coded] * len(SENT) + [plain] * len(KEPT),
        in_specs=[pl.BlockSpec(memory_space=pltpu.SMEM)] * 2 + [pl.BlockSpec(memory_space=pl.ANY)] * len(shares) + [pl.BlockSpec(memory_space=pltpu.HBM)],
        out_specs=[pl.BlockSpec(memory_space=pltpu.VMEM)] * len(SENT) + [pl.BlockSpec(memory_space=pl.ANY)] * len(KEPT),
        scratch_shapes=[
            pltpu.VMEM((blk_col, width, TILE), F32),
            pltpu.VMEM((len(shares) * size, width, TILE), jnp.bfloat16),
            pltpu.VMEM(tiles.shape, tiles.dtype),
            pltpu.VMEM((each, TILE), F32),
            pltpu.SemaphoreType.DMA((slots // CHUNK,)),
            pltpu.SemaphoreType.DMA((len(shares),)),
            pltpu.SemaphoreType.DMA((len(KEPT),)),
        ],
        compiler_params=params(40),
        name="backward",
    )(coords, info, *shares, tiles)


def spread_kernel(which, info, *refs):
    parts, (out_ref, scale, buffer, sem) = refs[: len(which)], refs[-4:]
    each = scale.shape[0]
    width = buffer.shape[1]
    size = each * TILE
    stores = []
    for k, (n, ref) in enumerate(zip(which, parts)):
        scale[...] = factor(ref[each * width :, :].astype(jnp.int32).astype(F32))
        for j in range(each):
            part = ref[j * width : (j + 1) * width, :].astype(jnp.int32).astype(F32)
            buffer[k, :, j * TILE : (j + 1) * TILE] = part * scale[j : j + 1, :]
        columns = pl.ds(pl.multiple_of(info[LINES + n] * size, size), size)
        stores.append(pltpu.make_async_copy(buffer.at[k], out_ref.at[:, columns], sem.at[k]))
        stores[-1].start()
    for store in stores:
        store.wait()


def spread(info, parts, width, which, out=None):
    rows = parts[0].shape[0]
    each = rows // (width + 1)
    vmem, hbm = pl.BlockSpec(memory_space=pltpu.VMEM), pl.BlockSpec(memory_space=pl.ANY)
    given = [] if out is None else [out]
    return pl.pallas_call(
        functools.partial(spread_kernel, which),
        out_shape=jax.ShapeDtypeStruct((width, len(HOPS) * each * TILE), F32),
        in_specs=[pl.BlockSpec(memory_space=pltpu.SMEM)] + [vmem] * len(which) + [hbm] * len(given),
        out_specs=hbm,
        scratch_shapes=[
            pltpu.VMEM((each, TILE), F32),
            pltpu.VMEM((len(which), width, each * TILE), F32),
            pltpu.SemaphoreType.DMA((len(which),)),
        ],
        input_output_aliases={1 + len(which): 0} if given else {},
        compiler_params=params(16),
        name="spread",
    )(info, *[parts[n] for n in which], *given)


def shift(value, axis, by):
    count = lax.axis_size(axis)
    return lax.ppermute(value, axis, [(i, (i + by) % count) for i in range(count)])


def gather(value, ring, pair, hold):
    across = shift(value, pair, 1)
    far = shift(value, ring, 2)
    up = shift(value, ring, 1)
    if hold:
        value, across = lax.optimization_barrier((value, across))
    down = shift(value, ring, -1)
    up_across = shift(across, ring, 1)
    down_across = shift(across, ring, -1)
    far_across = shift(far, pair, 1)
    return [value, across, up, down, up_across, down_across, far, far_across]


def numbers(ring, pair):
    i, j = lax.axis_index(ring), lax.axis_index(pair)
    return [lax.rem(i + a + 4, 4) * 2 + lax.rem(j + b, 2) for a, b in HOPS]


def scatter(sent, kept, ring, pair, last):
    far_across, up_across, down_across, up, down = sent
    own, across, far = kept
    far_across = shift(far_across, pair, 1)
    up_across = shift(up_across, ring, 1)
    down_across = shift(down_across, ring, -1)
    up = shift(up, ring, 1)
    down = shift(down, ring, -1)
    far = shift(merge(far, [far_across]), ring, 2)
    across = shift(merge(across, [up_across, down_across]), pair, 1)
    return last(own, [up, down, far, across])


def shards(tiles, tile_coords, tile_counts, omega):
    blocks = tiles[0, 0]
    coords = tile_coords[0, 0].T
    core = lax.axis_index("core")
    width = omega.shape[0]
    blk_col = omega.shape[1] // TILE
    rows = lax.axis_size(ROW)
    chips = lax.axis_size(CHIPS)
    blk_row = blk_col * 2 * chips // rows
    lines = [lax.rem(p, 2) * 4 + lax.div(p, 2) for p in numbers("z", "yh")]
    info = jnp.stack([tile_counts[0, 0], core, *numbers(*CHIPS), *lines])
    keep, give = forward(blocks, coords, info, omega, blk_row)
    got = shift(give, "core", 1)
    keep = plain(keep, width)
    sent = pair(info, keep, got, SENT[:FIRST], FIRST)
    rest = pair(info, keep, got, SENT[FIRST:] + KEPT, len(SENT) - FIRST)
    sent, kept = sent + rest[: len(SENT) - FIRST], rest[len(SENT) - FIRST :]
    mine = gather(scatter(sent, kept, *CHIPS, share), *CHIPS, True)
    early = lax.optimization_barrier([mine[n] for n in EARLY + (6,)])
    given = [*early[:-1], mine[4], mine[5], early[-1], mine[7]]
    theirs = [shift(value, "core", 1) for value in given]
    out = backward(blocks, coords, info, mine + theirs, blk_col)
    parts = gather(scatter(out[: len(SENT)], out[len(SENT) :], "z", "yh", merge), "z", "yh", False)
    return spread(info, parts, width, LATE, spread(info, parts, width, EARLY))


def solution(mesh):
    fine = Mesh(mesh.devices.reshape(2, 4, 4, 2, 2), ("yh", "z", "x", "yl", "core"))
    col = ("x", "yl", "core")
    return jax.shard_map(
        shards,
        mesh=fine,
        in_specs=(
            P(ROW, col, None, None, None),
            P(ROW, col, None, None),
            P(ROW, col),
            P(None, col),
        ),
        out_specs=P(None, col),
        check_vma=False,
    )
```

```python
import functools

import jax
import jax.numpy as jnp
from jax import lax
from jax.experimental import pallas as pl
from jax.experimental.pallas import tpu as pltpu
from jax.sharding import Mesh
from jax.sharding import PartitionSpec as P

TILE = 128
CHUNK = 64
UNROLL = 64
LAG = 8
BLOCKS = 32
LEVEL = 32700.0
STEPS = 8.0
MIB = 1024 * 1024
ROW = ("yh", "z")
CHIPS = ("x", "yl")
HOPS = [(0, 0), (0, 1), (-1, 0), (1, 0), (-1, 1), (1, 1), (2, 0), (2, 1)]
SENT = (7, 5, 4, 3, 2)
KEPT = (0, 1, 6)
FIRST = 3
EARLY = (0, 1, 2, 3, 6)
LATE = (4, 5, 7)
PLACES = 2
LINES = PLACES + len(HOPS)
F32 = jnp.float32
I16 = jnp.int16


def params(mib):
    return pltpu.CompilerParams(vmem_limit_bytes=mib * MIB)


def code(block):
    top = jnp.maximum(jnp.max(jnp.abs(block), axis=0, keepdims=True), 1e-30)
    step = jnp.ceil(jnp.log2(top) * STEPS)
    return step, jnp.exp2(step * (-1.0 / STEPS)) * LEVEL


def factor(step):
    return jnp.exp2(step * (1.0 / STEPS)) * (1.0 / LEVEL)


def put_blocks(read, count, out_ref, steps):
    rows = out_ref.shape[0] - count
    width = rows // count
    unroll = min(BLOCKS, count)

    def body(i, _):
        for u in range(unroll):
            j = i * unroll + u
            block = read(j)
            step, gain = code(block)
            whole = jnp.round(block * gain).astype(jnp.int32)
            out_ref[pl.ds(pl.multiple_of(j * width, width), width), :] = whole.astype(I16)
            steps[pl.ds(j, 1), :] = step
        return 0

    lax.fori_loop(0, count // unroll, body, 0)
    out_ref[rows:, :] = steps[:count].astype(jnp.int32).astype(I16)


def sparse_step(transposed, coords, base, source, tiles_ref, acc):
    def body(i, _):
        waiting = []
        for u in range(UNROLL + LAG):
            if u < UNROLL:
                slot = base + i * UNROLL + u
                r, c = coords[0, slot], coords[1, slot]
                if transposed:
                    left = source[:, pl.ds(pl.multiple_of(c * TILE, TILE), TILE)]
                    dims = (((1,), (1,)), ((), ()))
                    value = lax.dot_general(tiles_ref[slot], left, dims, preferred_element_type=F32)
                    waiting.append((r, value))
                else:
                    value = jnp.dot(source[r], tiles_ref[slot], preferred_element_type=F32)
                    waiting.append((c, value))
            if u >= LAG:
                target, value = waiting[u - LAG]
                acc[target] += value
        return 0

    lax.fori_loop(0, CHUNK // UNROLL, body, 0)


def fetch(count, tiles_ref, tiles, sem):
    def part(j):
        rows = pl.ds(j * CHUNK, CHUNK)
        return pltpu.make_async_copy(tiles_ref.at[rows], tiles.at[rows], sem.at[j])

    chunks = lax.div(count + (CHUNK - 1), CHUNK)
    lax.fori_loop(0, chunks, lambda j, _: (part(j).start(), 0)[1], 0)
    return chunks, part


def forward_kernel(coords, info, omega_ref, tiles_ref, keep_ref, give_ref, acc, omega, tiles, coded, steps, tile_sem, sem):
    half = acc.shape[0] // 2
    load = pltpu.make_async_copy(omega_ref, omega, sem.at[0])
    load.start()
    chunks, part = fetch(info[0], tiles_ref, tiles, tile_sem)
    acc[...] = jnp.zeros_like(acc)
    load.wait()

    def chunk(j, _):
        part(j).wait()
        sparse_step(True, coords, j * CHUNK, omega, tiles, acc)
        return 0

    lax.fori_loop(0, chunks, chunk, 0)
    core = info[1]
    keep = pltpu.make_async_copy(acc.at[pl.ds(core * half, half)], keep_ref, sem.at[1])
    keep.start()
    put_blocks(lambda j: acc[(1 - core) * half + j].T, half, coded, steps)
    give = pltpu.make_async_copy(coded, give_ref, sem.at[2])
    give.start()
    keep.wait()
    give.wait()


def forward(tiles, coords, info, omega, blk_row):
    slots = tiles.shape[0]
    width = omega.shape[0]
    half = blk_row // 2
    coded = jax.ShapeDtypeStruct((half * (width + 1), TILE), I16)
    return pl.pallas_call(
        forward_kernel,
        out_shape=(jax.ShapeDtypeStruct((half, TILE, width), F32), coded),
        in_specs=[pl.BlockSpec(memory_space=pltpu.SMEM)] * 2 + [pl.BlockSpec(memory_space=pltpu.HBM)] * 2,
        out_specs=[pl.BlockSpec(memory_space=pltpu.HBM)] * 2,
        scratch_shapes=[
            pltpu.VMEM((blk_row, TILE, width), F32),
            pltpu.VMEM(omega.shape, omega.dtype),
            pltpu.VMEM(tiles.shape, tiles.dtype),
            pltpu.VMEM(coded.shape, I16),
            pltpu.VMEM((half, TILE), F32),
            pltpu.SemaphoreType.DMA((slots // CHUNK,)),
            pltpu.SemaphoreType.DMA((3,)),
        ],
        compiler_params=params(60),
        name="forward",
    )(coords, info, omega, tiles)


def turn_kernel(which, info, in_ref, out_ref):
    each = out_ref.shape[1]
    for k, n in enumerate(which):
        first = info[PLACES + n] * each

        def body(j, _):
            out_ref[k, j] = in_ref[first + j].T
            return 0

        lax.fori_loop(0, each, body, 0, unroll=True)


def turn(info, blocks, which):
    count, rows, columns = blocks.shape
    return pl.pallas_call(
        functools.partial(turn_kernel, which),
        out_shape=jax.ShapeDtypeStruct((len(which), count // len(HOPS), columns, rows), F32),
        in_specs=[pl.BlockSpec(memory_space=pltpu.SMEM), pl.BlockSpec(memory_space=pltpu.VMEM)],
        out_specs=pl.BlockSpec(memory_space=pltpu.VMEM),
        compiler_params=params(14),
        name="turn",
    )(info, blocks)


def pair_kernel(which, sent, info, keep_ref, got_ref, *refs):
    outs, (scale, steps) = refs[:-2], refs[-2:]
    _, each, width, _ = keep_ref.shape
    blocks = each * len(HOPS)
    scales((got_ref,), scale, blocks * width)
    for k, (n, out_ref) in enumerate(zip(which, outs)):
        first = info[PLACES + n] * each

        def read(j):
            b = first + j
            got = got_ref[pl.ds(pl.multiple_of(b * width, width), width), :].astype(jnp.int32).astype(F32)
            return keep_ref[k, j] + got * scale[0, pl.ds(b, 1), :]

        if k < sent:
            put_blocks(read, each, out_ref, steps)
        else:

            def body(j, _):
                out_ref[j] = read(j)
                return 0

            lax.fori_loop(0, each, body, 0, unroll=8)


def pair(info, keep, got, which, sent):
    _, each, width, _ = keep.shape
    blocks = each * len(HOPS)
    coded = jax.ShapeDtypeStruct((each * width + each, TILE), I16)
    return pl.pallas_call(
        functools.partial(pair_kernel, which, sent),
        out_shape=[coded] * sent + [jax.ShapeDtypeStruct((each, width, TILE), F32)] * (len(which) - sent),
        in_specs=[pl.BlockSpec(memory_space=s) for s in (pltpu.SMEM, pltpu.VMEM, pltpu.VMEM)],
        out_specs=[pl.BlockSpec(memory_space=pltpu.VMEM)] * len(which),
        scratch_shapes=[pltpu.VMEM((1, blocks, TILE), F32), pltpu.VMEM((each, TILE), F32)],
        compiler_params=params(14),
        name="pair",
    )(info, keep, got)


def scales(parts, scale, rows):
    for n, ref in enumerate(parts):
        scale[n] = factor(ref[rows:, :].astype(jnp.int32).astype(F32))


def gather_sum(own_ref, parts, scale, j, width):
    total = own_ref[j]
    for n, ref in enumerate(parts):
        part = ref[pl.ds(pl.multiple_of(j * width, width), width), :].astype(jnp.int32).astype(F32)
        total = total + part * scale[n, pl.ds(j, 1), :]
    return total


def share_kernel(own_ref, *refs):
    parts, (out_ref, scale) = refs[:-2], refs[-2:]
    each, width, _ = own_ref.shape
    scales(parts, scale, each * width)

    def body(j, _):
        out_ref[j] = gather_sum(own_ref, parts, scale, j, width).astype(out_ref.dtype)
        return 0

    lax.fori_loop(0, each, body, 0, unroll=8)


def share(own, parts):
    each = own.shape[0]
    return pl.pallas_call(
        share_kernel,
        out_shape=jax.ShapeDtypeStruct(own.shape, jnp.bfloat16),
        scratch_shapes=[pltpu.VMEM((len(parts), each, TILE), F32)],
        compiler_params=params(12),
        name="share",
    )(own, *parts)


def merge_kernel(own_ref, *refs):
    parts, (out_ref, scale, steps) = refs[:-3], refs[-3:]
    each, width, _ = own_ref.shape
    scales(parts, scale, each * width)
    put_blocks(lambda j: gather_sum(own_ref, parts, scale, j, width), each, out_ref, steps)


def merge(own, parts):
    each = own.shape[0]
    return pl.pallas_call(
        merge_kernel,
        out_shape=jax.ShapeDtypeStruct(parts[0].shape, I16),
        scratch_shapes=[pltpu.VMEM((len(parts), each, TILE), F32), pltpu.VMEM((each, TILE), F32)],
        compiler_params=params(12),
        name="merge",
    )(own, *parts)


def backward_kernel(coords, info, *refs):
    acc, inner, tiles, steps, tile_sem, sem, out_sem = refs[-7:]
    count = inner.shape[0] // refs[0].shape[0]
    shares, tiles_ref, outs = refs[:count], refs[count], refs[count + 1 : -7]
    each = acc.shape[0] // len(outs)
    size = shares[0].shape[0]
    core = info[1]
    loads = []
    for n, ref in enumerate(shares):
        half = core if n < len(HOPS) else 1 - core
        place = half * len(HOPS) + info[PLACES + n % len(HOPS)]
        loads.append(pltpu.make_async_copy(ref, inner.at[pl.ds(place * size, size)], sem.at[n]))
        loads[-1].start()
    chunks, part = fetch(info[0], tiles_ref, tiles, tile_sem)
    acc[...] = jnp.zeros_like(acc)
    for load in loads:
        load.wait()

    def chunk(j, _):
        part(j).wait()
        sparse_step(False, coords, j * CHUNK, inner, tiles, acc)
        return 0

    lax.fori_loop(0, chunks, chunk, 0)
    stores = []
    for n, out_ref in zip(KEPT, outs[len(SENT) :]):
        first = info[LINES + n] * each
        stores.append(pltpu.make_async_copy(acc.at[pl.ds(first, each)], out_ref, out_sem.at[len(stores)]))
        stores[-1].start()
    for n, out_ref in zip(SENT, outs):
        first = info[LINES + n] * each
        put_blocks(lambda j: acc[first + j], each, out_ref, steps)
    for store in stores:
        store.wait()


def backward(tiles, coords, info, shares, blk_col):
    slots = tiles.shape[0]
    size, width, _ = shares[0].shape
    each = blk_col // len(HOPS)
    coded = jax.ShapeDtypeStruct((each * width + each, TILE), I16)
    plain = jax.ShapeDtypeStruct((each, width, TILE), F32)
    return pl.pallas_call(
        backward_kernel,
        out_shape=[coded] * len(SENT) + [plain] * len(KEPT),
        in_specs=[pl.BlockSpec(memory_space=pltpu.SMEM)] * 2 + [pl.BlockSpec(memory_space=pl.ANY)] * len(shares) + [pl.BlockSpec(memory_space=pltpu.HBM)],
        out_specs=[pl.BlockSpec(memory_space=pltpu.VMEM)] * len(SENT) + [pl.BlockSpec(memory_space=pl.ANY)] * len(KEPT),
        scratch_shapes=[
            pltpu.VMEM((blk_col, width, TILE), F32),
            pltpu.VMEM((len(shares) * size, width, TILE), jnp.bfloat16),
            pltpu.VMEM(tiles.shape, tiles.dtype),
            pltpu.VMEM((each, TILE), F32),
            pltpu.SemaphoreType.DMA((slots // CHUNK,)),
            pltpu.SemaphoreType.DMA((len(shares),)),
            pltpu.SemaphoreType.DMA((len(KEPT),)),
        ],
        compiler_params=params(40),
        name="backward",
    )(coords, info, *shares, tiles)


def spread_kernel(which, info, *refs):
    parts, (out_ref, scale, buffer, sem) = refs[: len(which)], refs[-4:]
    each = scale.shape[0]
    width = buffer.shape[1]
    size = each * TILE
    stores = []
    for k, (n, ref) in enumerate(zip(which, parts)):
        scale[...] = factor(ref[each * width :, :].astype(jnp.int32).astype(F32))
        for j in range(each):
            part = ref[j * width : (j + 1) * width, :].astype(jnp.int32).astype(F32)
            buffer[k, :, j * TILE : (j + 1) * TILE] = part * scale[j : j + 1, :]
        columns = pl.ds(pl.multiple_of(info[LINES + n] * size, size), size)
        stores.append(pltpu.make_async_copy(buffer.at[k], out_ref.at[:, columns], sem.at[k]))
        stores[-1].start()
    for store in stores:
        store.wait()


def spread(info, parts, width, which, out=None):
    rows = parts[0].shape[0]
    each = rows // (width + 1)
    vmem, hbm = pl.BlockSpec(memory_space=pltpu.VMEM), pl.BlockSpec(memory_space=pl.ANY)
    given = [] if out is None else [out]
    return pl.pallas_call(
        functools.partial(spread_kernel, which),
        out_shape=jax.ShapeDtypeStruct((width, len(HOPS) * each * TILE), F32),
        in_specs=[pl.BlockSpec(memory_space=pltpu.SMEM)] + [vmem] * len(which) + [hbm] * len(given),
        out_specs=hbm,
        scratch_shapes=[
            pltpu.VMEM((each, TILE), F32),
            pltpu.VMEM((len(which), width, each * TILE), F32),
            pltpu.SemaphoreType.DMA((len(which),)),
        ],
        input_output_aliases={1 + len(which): 0} if given else {},
        compiler_params=params(16),
        name="spread",
    )(info, *[parts[n] for n in which], *given)


def shift(value, axis, by):
    count = lax.axis_size(axis)
    return lax.ppermute(value, axis, [(i, (i + by) % count) for i in range(count)])


def gather(value, ring, pair, hold):
    across = shift(value, pair, 1)
    far = shift(value, ring, 2)
    up = shift(value, ring, 1)
    if hold:
        value, across = lax.optimization_barrier((value, across))
    down = shift(value, ring, -1)
    up_across = shift(across, ring, 1)
    down_across = shift(across, ring, -1)
    far_across = shift(far, pair, 1)
    return [value, across, up, down, up_across, down_across, far, far_across]


def numbers(ring, pair):
    i, j = lax.axis_index(ring), lax.axis_index(pair)
    return [lax.rem(i + a + 4, 4) * 2 + lax.rem(j + b, 2) for a, b in HOPS]


def scatter(sent, kept, ring, pair, last):
    far_across, up_across, down_across, up, down = sent
    own, across, far = kept
    far_across = shift(far_across, pair, 1)
    up_across = shift(up_across, ring, 1)
    down_across = shift(down_across, ring, -1)
    up = shift(up, ring, 1)
    down = shift(down, ring, -1)
    far = shift(merge(far, [far_across]), ring, 2)
    across = shift(merge(across, [up_across, down_across]), pair, 1)
    return last(own, [up, down, far, across])


def shards(tiles, tile_coords, tile_counts, omega):
    blocks = tiles[0, 0]
    coords = tile_coords[0, 0].T
    core = lax.axis_index("core")
    width = omega.shape[0]
    blk_col = omega.shape[1] // TILE
    rows = lax.axis_size(ROW)
    chips = lax.axis_size(CHIPS)
    blk_row = blk_col * 2 * chips // rows
    lines = [lax.rem(p, 2) * 4 + lax.div(p, 2) for p in numbers("z", "yh")]
    info = jnp.stack([tile_counts[0, 0], core, *numbers(*CHIPS), *lines])
    keep, give = forward(blocks, coords, info, omega, blk_row)
    got = shift(give, "core", 1)
    others = SENT[FIRST:] + KEPT
    sent = pair(info, turn(info, keep, SENT[:FIRST]), got, SENT[:FIRST], FIRST)
    rest = pair(info, turn(info, keep, others), got, others, len(SENT) - FIRST)
    sent, kept = sent + rest[: len(SENT) - FIRST], rest[len(SENT) - FIRST :]
    mine = gather(scatter(sent, kept, *CHIPS, share), *CHIPS, True)
    early = lax.optimization_barrier([mine[n] for n in EARLY])
    given = [*early[:-1], mine[4], mine[5], early[-1], mine[7]]
    theirs = [shift(value, "core", 1) for value in given]
    out = backward(blocks, coords, info, mine + theirs, blk_col)
    parts = gather(scatter(out[: len(SENT)], out[len(SENT) :], "z", "yh", merge), "z", "yh", False)
    return spread(info, parts, width, LATE, spread(info, parts, width, EARLY))


def solution(mesh):
    fine = Mesh(mesh.devices.reshape(2, 4, 4, 2, 2), ("yh", "z", "x", "yl", "core"))
    col = ("x", "yl", "core")
    return jax.shard_map(
        shards,
        mesh=fine,
        in_specs=(
            P(ROW, col, None, None, None),
            P(ROW, col, None, None),
            P(ROW, col),
            P(None, col),
        ),
        out_specs=P(None, col),
        check_vma=False,
    )
```

```python
import functools

import jax
import jax.numpy as jnp
from jax import lax
from jax.experimental import pallas as pl
from jax.experimental.pallas import tpu as pltpu
from jax.sharding import Mesh
from jax.sharding import PartitionSpec as P

TILE = 128
CHUNK = 64
UNROLL = 64
LAG = 8
BLOCKS = 64
LEVEL = 32700.0
STEPS = 8.0
MIB = 1024 * 1024
ROW = ("yh", "z")
CHIPS = ("x", "yl")
HOPS = [(0, 0), (0, 1), (-1, 0), (1, 0), (-1, 1), (1, 1), (2, 0), (2, 1)]
SENT = (7, 5, 4, 3, 2)
KEPT = (0, 1, 6)
FIRST = 3
EARLY = (0, 1, 2, 3, 6)
LATE = (4, 5, 7)
PLACES = 2
LINES = PLACES + len(HOPS)
F32 = jnp.float32
I16 = jnp.int16


def params(mib):
    return pltpu.CompilerParams(vmem_limit_bytes=mib * MIB)


def code(block):
    top = jnp.maximum(jnp.max(jnp.abs(block), axis=0, keepdims=True), 1e-30)
    step = jnp.ceil(jnp.log2(top) * STEPS)
    return step, jnp.exp2(step * (-1.0 / STEPS)) * LEVEL


def factor(step):
    return jnp.exp2(step * (1.0 / STEPS)) * (1.0 / LEVEL)


def put_blocks(read, count, out_ref, steps):
    rows = out_ref.shape[0] - count
    width = rows // count
    unroll = min(BLOCKS, count)

    def body(i, _):
        for u in range(unroll):
            j = i * unroll + u
            block = read(j)
            step, gain = code(block)
            whole = jnp.round(block * gain).astype(jnp.int32)
            out_ref[pl.ds(pl.multiple_of(j * width, width), width), :] = whole.astype(I16)
            steps[pl.ds(j, 1), :] = step
        return 0

    lax.fori_loop(0, count // unroll, body, 0)
    out_ref[rows:, :] = steps[:count].astype(jnp.int32).astype(I16)


def sparse_step(transposed, coords, base, source, tiles_ref, acc):
    def body(i, _):
        waiting = []
        for u in range(UNROLL + LAG):
            if u < UNROLL:
                slot = base + i * UNROLL + u
                r, c = coords[0, slot], coords[1, slot]
                if transposed:
                    left = source[:, pl.ds(pl.multiple_of(c * TILE, TILE), TILE)]
                    dims = (((1,), (1,)), ((), ()))
                    value = lax.dot_general(tiles_ref[slot], left, dims, preferred_element_type=F32)
                    waiting.append((r, value))
                else:
                    value = jnp.dot(source[r], tiles_ref[slot], preferred_element_type=F32)
                    waiting.append((c, value))
            if u >= LAG:
                target, value = waiting[u - LAG]
                acc[target] += value
        return 0

    lax.fori_loop(0, CHUNK // UNROLL, body, 0)


def fetch(count, tiles_ref, tiles, sem):
    def part(j):
        rows = pl.ds(j * CHUNK, CHUNK)
        return pltpu.make_async_copy(tiles_ref.at[rows], tiles.at[rows], sem.at[j])

    chunks = lax.div(count + (CHUNK - 1), CHUNK)
    lax.fori_loop(0, chunks, lambda j, _: (part(j).start(), 0)[1], 0)
    return chunks, part


def forward_kernel(coords, info, omega_ref, tiles_ref, keep_ref, give_ref, acc, omega, tiles, coded, steps, tile_sem, sem):
    half = acc.shape[0] // 2
    load = pltpu.make_async_copy(omega_ref, omega, sem.at[0])
    load.start()
    chunks, part = fetch(info[0], tiles_ref, tiles, tile_sem)
    acc[...] = jnp.zeros_like(acc)
    load.wait()

    def chunk(j, _):
        part(j).wait()
        sparse_step(True, coords, j * CHUNK, omega, tiles, acc)
        return 0

    lax.fori_loop(0, chunks, chunk, 0)
    core = info[1]
    keep = pltpu.make_async_copy(acc.at[pl.ds(core * half, half)], keep_ref, sem.at[1])
    keep.start()
    put_blocks(lambda j: acc[(1 - core) * half + j].T, half, coded, steps)
    give = pltpu.make_async_copy(coded, give_ref, sem.at[2])
    give.start()
    keep.wait()
    give.wait()


def forward(tiles, coords, info, omega, blk_row):
    slots = tiles.shape[0]
    width = omega.shape[0]
    half = blk_row // 2
    coded = jax.ShapeDtypeStruct((half * (width + 1), TILE), I16)
    return pl.pallas_call(
        forward_kernel,
        out_shape=(jax.ShapeDtypeStruct((half, TILE, width), F32), coded),
        in_specs=[pl.BlockSpec(memory_space=pltpu.SMEM)] * 2 + [pl.BlockSpec(memory_space=pltpu.HBM)] * 2,
        out_specs=[pl.BlockSpec(memory_space=pltpu.HBM)] * 2,
        scratch_shapes=[
            pltpu.VMEM((blk_row, TILE, width), F32),
            pltpu.VMEM(omega.shape, omega.dtype),
            pltpu.VMEM(tiles.shape, tiles.dtype),
            pltpu.VMEM(coded.shape, I16),
            pltpu.VMEM((half, TILE), F32),
            pltpu.SemaphoreType.DMA((slots // CHUNK,)),
            pltpu.SemaphoreType.DMA((3,)),
        ],
        compiler_params=params(60),
        name="forward",
    )(coords, info, omega, tiles)


def turn_kernel(which, info, in_ref, out_ref):
    each = out_ref.shape[1]
    for k, n in enumerate(which):
        first = info[PLACES + n] * each

        def body(j, _):
            out_ref[k, j] = in_ref[first + j].T
            return 0

        lax.fori_loop(0, each, body, 0, unroll=True)


def turn(info, blocks, which):
    count, rows, columns = blocks.shape
    return pl.pallas_call(
        functools.partial(turn_kernel, which),
        out_shape=jax.ShapeDtypeStruct((len(which), count // len(HOPS), columns, rows), F32),
        in_specs=[pl.BlockSpec(memory_space=pltpu.SMEM), pl.BlockSpec(memory_space=pltpu.VMEM)],
        out_specs=pl.BlockSpec(memory_space=pltpu.VMEM),
        compiler_params=params(14),
        name="turn",
    )(info, blocks)


def pair_kernel(which, sent, info, keep_ref, got_ref, *refs):
    outs, (scale, steps) = refs[:-2], refs[-2:]
    _, each, width, _ = keep_ref.shape
    blocks = each * len(HOPS)
    scales((got_ref,), scale, blocks * width)
    for k, (n, out_ref) in enumerate(zip(which, outs)):
        first = info[PLACES + n] * each

        def read(j):
            b = first + j
            got = got_ref[pl.ds(pl.multiple_of(b * width, width), width), :].astype(jnp.int32).astype(F32)
            return keep_ref[k, j] + got * scale[0, pl.ds(b, 1), :]

        if k < sent:
            put_blocks(read, each, out_ref, steps)
        else:

            def body(j, _):
                out_ref[j] = read(j)
                return 0

            lax.fori_loop(0, each, body, 0, unroll=8)


def pair(info, keep, got, which, sent):
    _, each, width, _ = keep.shape
    blocks = each * len(HOPS)
    coded = jax.ShapeDtypeStruct((each * width + each, TILE), I16)
    return pl.pallas_call(
        functools.partial(pair_kernel, which, sent),
        out_shape=[coded] * sent + [jax.ShapeDtypeStruct((each, width, TILE), F32)] * (len(which) - sent),
        in_specs=[pl.BlockSpec(memory_space=s) for s in (pltpu.SMEM, pltpu.VMEM, pltpu.VMEM)],
        out_specs=[pl.BlockSpec(memory_space=pltpu.VMEM)] * len(which),
        scratch_shapes=[pltpu.VMEM((1, blocks, TILE), F32), pltpu.VMEM((each, TILE), F32)],
        compiler_params=params(14),
        name="pair",
    )(info, keep, got)


def scales(parts, scale, rows):
    for n, ref in enumerate(parts):
        scale[n] = factor(ref[rows:, :].astype(jnp.int32).astype(F32))


def gather_sum(own_ref, parts, scale, j, width):
    total = own_ref[j]
    for n, ref in enumerate(parts):
        part = ref[pl.ds(pl.multiple_of(j * width, width), width), :].astype(jnp.int32).astype(F32)
        total = total + part * scale[n, pl.ds(j, 1), :]
    return total


def share_kernel(own_ref, *refs):
    parts, (out_ref, scale) = refs[:-2], refs[-2:]
    each, width, _ = own_ref.shape
    scales(parts, scale, each * width)

    def body(j, _):
        out_ref[j] = gather_sum(own_ref, parts, scale, j, width).astype(out_ref.dtype)
        return 0

    lax.fori_loop(0, each, body, 0, unroll=8)


def share(own, parts):
    each = own.shape[0]
    return pl.pallas_call(
        share_kernel,
        out_shape=jax.ShapeDtypeStruct(own.shape, jnp.bfloat16),
        scratch_shapes=[pltpu.VMEM((len(parts), each, TILE), F32)],
        compiler_params=params(12),
        name="share",
    )(own, *parts)


def merge_kernel(own_ref, *refs):
    parts, (out_ref, scale, steps) = refs[:-3], refs[-3:]
    each, width, _ = own_ref.shape
    scales(parts, scale, each * width)
    put_blocks(lambda j: gather_sum(own_ref, parts, scale, j, width), each, out_ref, steps)


def merge(own, parts):
    each = own.shape[0]
    return pl.pallas_call(
        merge_kernel,
        out_shape=jax.ShapeDtypeStruct(parts[0].shape, I16),
        scratch_shapes=[pltpu.VMEM((len(parts), each, TILE), F32), pltpu.VMEM((each, TILE), F32)],
        compiler_params=params(12),
        name="merge",
    )(own, *parts)


def backward_kernel(coords, info, *refs):
    acc, inner, tiles, steps, tile_sem, sem, out_sem = refs[-7:]
    count = inner.shape[0] // refs[0].shape[0]
    shares, tiles_ref, outs = refs[:count], refs[count], refs[count + 1 : -7]
    each = acc.shape[0] // len(outs)
    size = shares[0].shape[0]
    core = info[1]
    loads = []
    for n, ref in enumerate(shares):
        half = core if n < len(HOPS) else 1 - core
        place = half * len(HOPS) + info[PLACES + n % len(HOPS)]
        loads.append(pltpu.make_async_copy(ref, inner.at[pl.ds(place * size, size)], sem.at[n]))
        loads[-1].start()
    chunks, part = fetch(info[0], tiles_ref, tiles, tile_sem)
    acc[...] = jnp.zeros_like(acc)
    for load in loads:
        load.wait()

    def chunk(j, _):
        part(j).wait()
        sparse_step(False, coords, j * CHUNK, inner, tiles, acc)
        return 0

    lax.fori_loop(0, chunks, chunk, 0)
    stores = []
    for n, out_ref in zip(KEPT, outs[len(SENT) :]):
        first = info[LINES + n] * each
        stores.append(pltpu.make_async_copy(acc.at[pl.ds(first, each)], out_ref, out_sem.at[len(stores)]))
        stores[-1].start()
    for n, out_ref in zip(SENT, outs):
        first = info[LINES + n] * each
        put_blocks(lambda j: acc[first + j], each, out_ref, steps)
    for store in stores:
        store.wait()


def backward(tiles, coords, info, shares, blk_col):
    slots = tiles.shape[0]
    size, width, _ = shares[0].shape
    each = blk_col // len(HOPS)
    coded = jax.ShapeDtypeStruct((each * width + each, TILE), I16)
    plain = jax.ShapeDtypeStruct((each, width, TILE), F32)
    return pl.pallas_call(
        backward_kernel,
        out_shape=[coded] * len(SENT) + [plain] * len(KEPT),
        in_specs=[pl.BlockSpec(memory_space=pltpu.SMEM)] * 2 + [pl.BlockSpec(memory_space=pl.ANY)] * len(shares) + [pl.BlockSpec(memory_space=pltpu.HBM)],
        out_specs=[pl.BlockSpec(memory_space=pltpu.VMEM)] * len(SENT) + [pl.BlockSpec(memory_space=pl.ANY)] * len(KEPT),
        scratch_shapes=[
            pltpu.VMEM((blk_col, width, TILE), F32),
            pltpu.VMEM((len(shares) * size, width, TILE), jnp.bfloat16),
            pltpu.VMEM(tiles.shape, tiles.dtype),
            pltpu.VMEM((each, TILE), F32),
            pltpu.SemaphoreType.DMA((slots // CHUNK,)),
            pltpu.SemaphoreType.DMA((len(shares),)),
            pltpu.SemaphoreType.DMA((len(KEPT),)),
        ],
        compiler_params=params(40),
        name="backward",
    )(coords, info, *shares, tiles)


def spread_kernel(which, info, *refs):
    parts, (out_ref, scale, buffer, sem) = refs[: len(which)], refs[-4:]
    each = scale.shape[0]
    width = buffer.shape[1]
    size = each * TILE
    stores = []
    for k, (n, ref) in enumerate(zip(which, parts)):
        scale[...] = factor(ref[each * width :, :].astype(jnp.int32).astype(F32))
        for j in range(each):
            part = ref[j * width : (j + 1) * width, :].astype(jnp.int32).astype(F32)
            buffer[k, :, j * TILE : (j + 1) * TILE] = part * scale[j : j + 1, :]
        columns = pl.ds(pl.multiple_of(info[LINES + n] * size, size), size)
        stores.append(pltpu.make_async_copy(buffer.at[k], out_ref.at[:, columns], sem.at[k]))
        stores[-1].start()
    for store in stores:
        store.wait()


def spread(info, parts, width, which, out=None):
    rows = parts[0].shape[0]
    each = rows // (width + 1)
    vmem, hbm = pl.BlockSpec(memory_space=pltpu.VMEM), pl.BlockSpec(memory_space=pl.ANY)
    given = [] if out is None else [out]
    return pl.pallas_call(
        functools.partial(spread_kernel, which),
        out_shape=jax.ShapeDtypeStruct((width, len(HOPS) * each * TILE), F32),
        in_specs=[pl.BlockSpec(memory_space=pltpu.SMEM)] + [vmem] * len(which) + [hbm] * len(given),
        out_specs=hbm,
        scratch_shapes=[
            pltpu.VMEM((each, TILE), F32),
            pltpu.VMEM((len(which), width, each * TILE), F32),
            pltpu.SemaphoreType.DMA((len(which),)),
        ],
        input_output_aliases={1 + len(which): 0} if given else {},
        compiler_params=params(16),
        name="spread",
    )(info, *[parts[n] for n in which], *given)


def shift(value, axis, by):
    count = lax.axis_size(axis)
    return lax.ppermute(value, axis, [(i, (i + by) % count) for i in range(count)])


def gather(value, ring, pair, hold):
    across = shift(value, pair, 1)
    far = shift(value, ring, 2)
    up = shift(value, ring, 1)
    if hold:
        value, across = lax.optimization_barrier((value, across))
    down = shift(value, ring, -1)
    up_across = shift(across, ring, 1)
    down_across = shift(across, ring, -1)
    far_across = shift(far, pair, 1)
    return [value, across, up, down, up_across, down_across, far, far_across]


def numbers(ring, pair):
    i, j = lax.axis_index(ring), lax.axis_index(pair)
    return [lax.rem(i + a + 4, 4) * 2 + lax.rem(j + b, 2) for a, b in HOPS]


def scatter(sent, kept, ring, pair, last):
    far_across, up_across, down_across, up, down = sent
    own, across, far = kept
    far_across = shift(far_across, pair, 1)
    up_across = shift(up_across, ring, 1)
    down_across = shift(down_across, ring, -1)
    up = shift(up, ring, 1)
    down = shift(down, ring, -1)
    far = shift(merge(far, [far_across]), ring, 2)
    across = shift(merge(across, [up_across, down_across]), pair, 1)
    return last(own, [up, down, far, across])


def shards(tiles, tile_coords, tile_counts, omega):
    blocks = tiles[0, 0]
    coords = tile_coords[0, 0].T
    core = lax.axis_index("core")
    width = omega.shape[0]
    blk_col = omega.shape[1] // TILE
    rows = lax.axis_size(ROW)
    chips = lax.axis_size(CHIPS)
    blk_row = blk_col * 2 * chips // rows
    lines = [lax.rem(p, 2) * 4 + lax.div(p, 2) for p in numbers("z", "yh")]
    info = jnp.stack([tile_counts[0, 0], core, *numbers(*CHIPS), *lines])
    keep, give = forward(blocks, coords, info, omega, blk_row)
    got = shift(give, "core", 1)
    others = SENT[FIRST:] + KEPT
    sent = pair(info, turn(info, keep, SENT[:FIRST]), got, SENT[:FIRST], FIRST)
    rest = pair(info, turn(info, keep, others), got, others, len(SENT) - FIRST)
    sent, kept = sent + rest[: len(SENT) - FIRST], rest[len(SENT) - FIRST :]
    mine = gather(scatter(sent, kept, *CHIPS, share), *CHIPS, True)
    own, across, up, far, far_across = lax.optimization_barrier([mine[n] for n in (0, 1, 3, 6, 7)])
    given = [own, across, mine[2], up, mine[4], mine[5], far, far_across]
    theirs = [shift(value, "core", 1) for value in given]
    out = backward(blocks, coords, info, mine + theirs, blk_col)
    parts = gather(scatter(out[: len(SENT)], out[len(SENT) :], "z", "yh", merge), "z", "yh", False)
    return spread(info, parts, width, LATE, spread(info, parts, width, EARLY))


def solution(mesh):
    fine = Mesh(mesh.devices.reshape(2, 4, 4, 2, 2), ("yh", "z", "x", "yl", "core"))
    col = ("x", "yl", "core")
    return jax.shard_map(
        shards,
        mesh=fine,
        in_specs=(
            P(ROW, col, None, None, None),
            P(ROW, col, None, None),
            P(ROW, col),
            P(None, col),
        ),
        out_specs=P(None, col),
        check_vma=False,
    )
```
